32 devices in a mesh: tm: 2 (over y), space: 16 (over z, x, core).
Axes of the slice: x: 2, y: 2, z: 4, core: 2. Of those that a mesh axis runs over, the one named last changes fastest.
Arguments:
- snapshots: bfloat16 [128, 128, 4096], P('tm', None, 'space'), as said below
- frequencies: int32 [4], replicated, may hold values from 1 to 63, as said below
- offsets: int32 [128], P('tm'), may hold values from 0 to 16383
Outputs:
- modes: float32 [4, 2, 128, 4096], P('tm', None, None, 'space')
The draws below stay inside these ranges and needn't reach their ends.
Inputs may be any that keep to these rules, and one draw needn't show every extreme that they name: `frequencies`: the kept frequency indices are distinct and include 1 and 63. `snapshots`: snapshot values of the record.
All inputs are finite; a program needn't handle non-finite values.
Results may differ from the reference program's by a relative error of at most 0.0041.
Values may be sent and summed in bfloat16 or wider, within the bound.
No kernel may reach another device: no remote copies, remote signals or barrier semaphores. Data moves between devices by JAX's collectives and lax.ppermute only.
A program may use at most 64 MiB of HBM per device.

```python
import math
import jax
import jax.numpy as jnp
from jax import lax

NB = 128
NFFT = 128
NF = 4
NCELLS = 4096


def draw_snapshots(key, part):
    keys = jax.random.split(key, 3)
    position = jnp.arange(NCELLS, dtype=jnp.float32) / NCELLS
    cell_scale = 0.3 * jnp.exp(math.log(10.0) * position) * jnp.exp(jax.random.uniform(keys[0], (NCELLS,), jnp.float32, math.log(0.7), math.log(1.4)))
    block_scale = jnp.exp(jax.random.uniform(keys[1], (NB,), jnp.float32, math.log(0.3), math.log(3.0)))
    base = jax.random.normal(keys[2], (NB, NFFT, NCELLS), jnp.float32)
    values = base * block_scale[:, None, None] * cell_scale[None, None, :]
    return values.astype(jnp.bfloat16)


def draw_frequencies(key, part):
    first_key = jax.random.fold_in(key, 11)
    second_key = jax.random.fold_in(key, 12)
    middle = jax.random.permutation(first_key, jnp.arange(2, NFFT // 2 - 1, dtype=jnp.int32))[:NF - 2]
    chosen = jnp.concatenate([jnp.array([1, NFFT // 2 - 1], dtype=jnp.int32), middle])
    shuffle_order = jax.random.permutation(second_key, jnp.arange(NF, dtype=jnp.int32))
    return chosen[shuffle_order]


def plant(result, stream_key, low, top_value):
    longest = result.shape.index(max(result.shape))
    spots = []
    for shift in (0, 1):
        where = [jax.random.randint(jax.random.fold_in(stream_key, axis), (), 0, length) for axis, length in enumerate(result.shape)]
        where[longest] = (where[longest] + shift) % result.shape[longest]
        spots.append(tuple(where))
    return result.at[spots[0]].set(low).at[spots[1]].set(top_value)


def setup_inputs(seed: int = 0) -> dict:
    streams_of = jax.random.split(jax.random.key(seed), 4)
    snapshots = draw_snapshots(jax.random.fold_in(streams_of[3], 71), 0)
    frequencies = draw_frequencies(jax.random.fold_in(streams_of[3], 71), 0)
    offsets = plant(jax.random.randint(streams_of[2], (NB,), 0, NFFT * NB), jax.random.fold_in(streams_of[2], 1), 0, (NFFT * NB) - 1).astype(jnp.int32)
    return {"snapshots": snapshots, "frequencies": frequencies, "offsets": offsets}


def make_angle_table(frequencies, length):
    positions = jnp.arange(length, dtype=jnp.int32)
    turn_counts = frequencies[None, :] * positions[:, None] % length
    radians = turn_counts.astype(jnp.float32) * (2.0 * math.pi / length)
    window = 0.5 - 0.5 * jnp.cos(positions.astype(jnp.float32) * (2.0 * math.pi / length))
    cosine_cols = window[:, None] * jnp.cos(radians)
    sine_cols = window[:, None] * jnp.sin(radians)
    return jnp.concatenate([cosine_cols, sine_cols], axis=1).astype(jnp.bfloat16)

def embed_gram(gram_real, gram_imag):
    top_rows = jnp.stack([gram_real, -gram_imag], axis=-1)
    low_rows = jnp.stack([gram_imag, gram_real], axis=-1)
    order = gram_real.shape[0]
    return jnp.stack([top_rows, low_rows], axis=1).reshape(2 * order, 2 * order)

def reference(snapshots, frequencies, offsets):
    angle_table = make_angle_table(frequencies, NFFT)
    table_rows = angle_table.T

    def one_block(block_pair):
        block_data, block_start = block_pair
        projected = jnp.dot(table_rows.astype(jnp.float32), block_data.astype(jnp.float32), preferred_element_type=jnp.float32)
        cos_part = projected[:NF]
        sin_part = projected[NF:]
        turn_counts = frequencies * block_start % NFFT
        phase = turn_counts.astype(jnp.float32) * (2.0 * math.pi / NFFT)
        cos_phase = jnp.cos(phase)[:, None]
        sin_phase = jnp.sin(phase)[:, None]
        real_part = cos_part * cos_phase - sin_part * sin_phase
        imag_part = -(sin_part * cos_phase + cos_part * sin_phase)
        return jnp.stack([real_part, imag_part]).astype(jnp.bfloat16)
    coeffs = lax.map(one_block, (snapshots, offsets))

    def one_freq(slot_index):
        picked = lax.dynamic_index_in_dim(coeffs, slot_index, axis=2, keepdims=False)
        real_rows = picked[:, 0]
        imag_rows = picked[:, 1]
        real_gram = jnp.dot(real_rows.astype(jnp.float32), real_rows.T.astype(jnp.float32), preferred_element_type=jnp.float32) + jnp.dot(imag_rows.astype(jnp.float32), imag_rows.T.astype(jnp.float32), preferred_element_type=jnp.float32)
        cross = jnp.dot(imag_rows.astype(jnp.float32), real_rows.T.astype(jnp.float32), preferred_element_type=jnp.float32)
        imag_gram = cross - cross.T
        embedded = embed_gram(real_gram / NCELLS, imag_gram / NCELLS)
        lower_factor = jnp.linalg.cholesky(embedded)
        stacked_rows = jnp.stack([real_rows, imag_rows], axis=1).reshape(2 * NB, NCELLS).astype(jnp.float32)
        solved = lax.linalg.triangular_solve(lower_factor, stacked_rows, left_side=True, lower=True)
        return jnp.transpose(solved.reshape(NB, 2, NCELLS), (1, 0, 2))
    return lax.map(one_freq, jnp.arange(NF, dtype=jnp.int32))
```

```python
import functools
import math

import jax
import jax.numpy as jnp
from jax import lax
from jax.experimental import pallas as pl
from jax.experimental.pallas import tpu as pltpu
from jax.sharding import PartitionSpec as P

TILE = 8
CHUNK = 16
VMEM_LIMIT = 48 * 1024 * 1024


def whole_vmem(count):
    return [pl.BlockSpec(memory_space=pltpu.VMEM)] * count


def rows_of(shape):
    return lax.broadcasted_iota(jnp.int32, shape, 0)


def lanes_of(shape):
    return lax.broadcasted_iota(jnp.int32, shape, 1)


def project_kernel(groups, freq_ref, offset_ref, snap_ref, *refs):
    outs, (held, sems) = refs[:groups], refs[groups:]
    blocks, length, cells = snap_ref.shape
    chunks = blocks // CHUNK
    copies = []
    for step in range(chunks):
        part = pl.ds(step * CHUNK, CHUNK)
        copies.append(pltpu.make_async_copy(snap_ref.at[part], held.at[part], sems.at[step]))
        copies[-1].start()

    count = freq_ref.shape[0]
    per_group = count // groups
    first = lax.axis_index("tm") * per_group if groups > 1 else 0
    picked = [freq_ref[lax.rem(first + j, count)] for j in range(count)]

    def turned(moments):
        row = rows_of((2 * count, moments.shape[1]))
        freq = jnp.zeros(row.shape, jnp.int32)
        for j in range(count):
            freq = jnp.where((row == j) | (row == j + count), picked[j], freq)
        turns = lax.rem(freq * moments, length)
        turns = jnp.where(row >= count, turns - length // 4, turns)
        return jnp.cos(turns.astype(jnp.float32) * (2.0 * math.pi / length))

    moments = lanes_of((2 * count, length))
    window = 0.5 - 0.5 * jnp.cos(moments.astype(jnp.float32) * (2.0 * math.pi / length))
    table = window * turned(moments)
    tile_row = rows_of((TILE, length))
    table_rows = []
    for j in range(2 * count):
        spread = jnp.broadcast_to(table[j : j + 1, :], (TILE, length))
        table_rows.append(
            jnp.concatenate([jnp.where(tile_row == b, spread, 0.0) for b in range(TILE)], axis=1)
        )
    spread_table = jnp.concatenate(table_rows, axis=0).astype(jnp.bfloat16)
    phases = turned(jnp.broadcast_to(offset_ref[...], (2 * count, blocks))).T

    for step in range(chunks):
        copies[step].wait()
        parts = []
        for half in range(CHUNK // TILE):
            start = step * CHUNK + half * TILE
            data = held[start : start + TILE].reshape(TILE * length, cells)
            projected = jnp.dot(spread_table, data, preferred_element_type=jnp.float32)
            turn = phases[start : start + TILE]
            pairs = []
            for j in range(count):
                cos_part = projected[j * TILE : (j + 1) * TILE]
                sin_part = projected[(count + j) * TILE : (count + j + 1) * TILE]
                cos_phase = turn[:, j : j + 1]
                sin_phase = turn[:, count + j : count + j + 1]
                pairs.append(
                    (
                        cos_part * cos_phase - sin_part * sin_phase,
                        -(sin_part * cos_phase + cos_part * sin_phase),
                    )
                )
            parts.append(pairs)
        for j in range(count):
            for p in range(2):
                value = jnp.concatenate([pairs[j][p] for pairs in parts], axis=0)
                target = outs[j // per_group]
                target[j % per_group, p, step * CHUNK : (step + 1) * CHUNK, :] = value.astype(
                    jnp.bfloat16
                )


def project(snapshots, frequencies, offsets, groups):
    blocks, length, cells = snapshots.shape
    count = frequencies.shape[0]
    shape = jax.ShapeDtypeStruct((count // groups, 2, blocks, cells), jnp.bfloat16)
    return pl.pallas_call(
        functools.partial(project_kernel, groups),
        out_shape=[shape] * groups,
        in_specs=[
            pl.BlockSpec(memory_space=pltpu.SMEM),
            pl.BlockSpec(memory_space=pltpu.VMEM),
            pl.BlockSpec(memory_space=pl.ANY),
        ],
        out_specs=whole_vmem(groups),
        scratch_shapes=[
            pltpu.VMEM(snapshots.shape, snapshots.dtype),
            pltpu.SemaphoreType.DMA((blocks // CHUNK,)),
        ],
        compiler_params=pltpu.CompilerParams(vmem_limit_bytes=VMEM_LIMIT),
        name="project",
    )(frequencies, offsets.reshape(1, blocks), snapshots)


def gram_kernel(halves, scale, *refs):
    pieces = refs[: 2 * halves]
    held_ref, keep_ref, send_ref, other, packed = refs[2 * halves :]
    count = held_ref.shape[0]
    order = held_ref.shape[2]
    first = lax.axis_index("tm") if halves > 1 else 0
    size = order // halves
    for s, target in ((0, held_ref), (1, other)):
        for h in range(halves):
            place = pl.ds(pl.multiple_of(lax.rem(first + h, halves) * size, size), size)
            target[:, :, place, :] = pieces[s * halves + h][...]
    lower = rows_of((order, order)) >= lanes_of((order, order))
    turn = (((1,), (1,)), ((), ()))
    for f in range(count):
        real = jnp.concatenate([held_ref[f, 0], other[f, 0]], axis=1)
        imag = jnp.concatenate([held_ref[f, 1], other[f, 1]], axis=1)
        both = jnp.concatenate([real, imag], axis=1)
        crossed = jnp.concatenate([imag, -real], axis=1)
        gram_real = lax.dot_general(both, both, turn, preferred_element_type=jnp.float32)
        gram_imag = lax.dot_general(crossed, both, turn, preferred_element_type=jnp.float32)
        packed[f] = jnp.where(lower, gram_real, gram_imag) * scale
    bit = lax.rem(lax.axis_index("space"), 2)
    part = count // 2
    keep_ref[...] = packed[pl.ds(bit * part, part)]
    send_ref[...] = packed[pl.ds((1 - bit) * part, part)]


def gram(pieces, halves, scale):
    count, _, size, cells = pieces[0].shape
    order = size * halves
    held = jax.ShapeDtypeStruct((count, 2, order, cells), jnp.bfloat16)
    half = jax.ShapeDtypeStruct((count // 2, order, order), jnp.float32)
    return pl.pallas_call(
        functools.partial(gram_kernel, halves, scale),
        out_shape=[held, half, half],
        in_specs=whole_vmem(len(pieces)),
        out_specs=whole_vmem(3),
        scratch_shapes=[
            pltpu.VMEM(held.shape, held.dtype),
            pltpu.VMEM((count, order, order), jnp.float32),
        ],
        compiler_params=pltpu.CompilerParams(vmem_limit_bytes=VMEM_LIMIT),
        name="gram",
    )(*pieces)


def spread_row(tile, p):
    return jnp.broadcast_to(tile[p : p + 1, :], tile.shape)


def spread_lane(tile, p):
    return jnp.broadcast_to(tile[:, p : p + 1], tile.shape)


def invert_factor(packed, out_ref, slot):
    order = packed.shape[0]
    shape = (TILE, order)
    tiles = order // TILE
    flipped = packed.T
    row, lane = rows_of((order, order)), lanes_of((order, order))
    full_real = jnp.where(row >= lane, packed, flipped)
    full_imag = jnp.where(row < lane, packed, jnp.where(row == lane, 0.0, -flipped))
    real = [full_real[t * TILE : (t + 1) * TILE] for t in range(tiles)]
    imag = [full_imag[t * TILE : (t + 1) * TILE] for t in range(tiles)]
    tile_row, tile_lane = rows_of(shape), lanes_of(shape)
    at_row = [tile_row == p for p in range(TILE)]
    for k in range(tiles):
        base = k * TILE
        inside = (tile_lane >= base) & (tile_lane < base + TILE)
        col_real = [spread_lane(real[k], base + q) for q in range(TILE)]
        col_imag = [spread_lane(imag[k], base + q) for q in range(TILE)]
        here_real = jnp.where(inside, jnp.where(tile_lane == base + tile_row, 1.0, 0.0), real[k])
        here_imag = jnp.where(inside, 0.0, imag[k])
        done_real, done_imag = here_real, here_imag
        for p in range(TILE):
            pivot = spread_row(col_real[p], p)
            inverse = 1.0 / pivot
            root = lax.rsqrt(pivot)
            done_real = jnp.where(at_row[p], here_real * root, done_real)
            done_imag = jnp.where(at_row[p], here_imag * root, done_imag)
            lead_real, lead_imag = col_real[p], col_imag[p]

            def eliminate(a_real, a_imag):
                top_real = spread_row(a_real, p) * inverse
                top_imag = spread_row(a_imag, p) * inverse
                new_real = a_real - (lead_real * top_real - lead_imag * top_imag)
                new_imag = a_imag - (lead_real * top_imag + lead_imag * top_real)
                return (
                    jnp.where(at_row[p], top_real, new_real),
                    jnp.where(at_row[p], top_imag, new_imag),
                )

            for q in range(p + 1, TILE):
                col_real[q], col_imag[q] = eliminate(col_real[q], col_imag[q])
            here_real, here_imag = eliminate(here_real, here_imag)
        keep = tile_lane < base + TILE
        out_ref[slot, 0, base : base + TILE, :] = jnp.where(keep, done_real, 0.0)
        out_ref[slot, 1, base : base + TILE, :] = jnp.where(keep, done_imag, 0.0)
        if k + 1 < tiles:
            rows_real = [spread_row(here_real, p) for p in range(TILE)]
            rows_imag = [spread_row(here_imag, p) for p in range(TILE)]
        for t in range(k + 1, tiles):
            a_real = jnp.where(inside, 0.0, real[t])
            a_imag = jnp.where(inside, 0.0, imag[t])
            for p in range(TILE):
                lead_real = spread_lane(real[t], base + p)
                lead_imag = spread_lane(imag[t], base + p)
                a_real = a_real - lead_real * rows_real[p] + lead_imag * rows_imag[p]
                a_imag = a_imag - lead_real * rows_imag[p] - lead_imag * rows_real[p]
            real[t], imag[t] = a_real, a_imag


def factor_kernel(terms, *refs):
    out_ref = refs[terms]
    total = refs[0][...]
    for r in refs[1:terms]:
        total = total + r[...]
    for slot in range(total.shape[0]):
        invert_factor(total[slot], out_ref, slot)


def factor(terms):
    count, order, _ = terms[0].shape
    return pl.pallas_call(
        functools.partial(factor_kernel, len(terms)),
        out_shape=jax.ShapeDtypeStruct((count, 2, order, order), jnp.float32),
        in_specs=whole_vmem(len(terms)),
        out_specs=pl.BlockSpec(memory_space=pltpu.VMEM),
        compiler_params=pltpu.CompilerParams(vmem_limit_bytes=VMEM_LIMIT),
        name="factor",
    )(*terms)


def apply_kernel(own_ref, sent_ref, held_ref, out_ref):
    part = own_ref.shape[0]
    order = held_ref.shape[2]
    bit = lax.rem(lax.axis_index("space"), 2)
    for which, source in ((bit, own_ref), (1 - bit, sent_ref)):
        for slot in range(part):
            f = which * part + slot
            real, imag = source[slot, 0], source[slot, 1]
            full = jnp.concatenate(
                [
                    jnp.concatenate([real, -imag], axis=1),
                    jnp.concatenate([imag, real], axis=1),
                ],
                axis=0,
            )
            high = full.astype(jnp.bfloat16)
            low = (full - high.astype(jnp.float32)).astype(jnp.bfloat16)
            data = held_ref[f].reshape(2 * order, held_ref.shape[3])
            value = jnp.dot(high, data, preferred_element_type=jnp.float32) + jnp.dot(
                low, data, preferred_element_type=jnp.float32
            )
            out_ref[f] = value.reshape(held_ref.shape[1:])


def apply(own, sent, held):
    return pl.pallas_call(
        apply_kernel,
        out_shape=jax.ShapeDtypeStruct(held.shape, jnp.float32),
        in_specs=whole_vmem(3),
        out_specs=pl.BlockSpec(memory_space=pltpu.VMEM),
        compiler_params=pltpu.CompilerParams(vmem_limit_bytes=VMEM_LIMIT),
        name="apply",
    )(own, sent, held)


def swap(value, size, mask):
    return lax.ppermute(value, "space", [(i, i ^ mask) for i in range(size)])


def swap_both(value, size, mask):
    pairs = [(t * size + i, (1 - t) * size + (i ^ mask)) for t in range(2) for i in range(size)]
    return lax.ppermute(value, ("tm", "space"), pairs)


def local(snapshots, frequencies, offsets):
    halves = lax.axis_size("tm")
    size = lax.axis_size("space")
    scale = 1.0 / (snapshots.shape[2] * size)
    if halves == 2:
        mine, theirs = project(snapshots, frequencies, offsets, 2)
        pieces = [
            mine,
            swap_both(theirs, size, 0),
            swap(mine, size, 2),
            swap_both(theirs, size, 2),
        ]
        held, keep, send = gram(pieces, 2, scale)
    else:
        (coeffs,) = project(snapshots, frequencies, offsets, 1)
        regrouped = lax.all_to_all(coeffs, "tm", split_axis=0, concat_axis=2, tiled=True)
        held, keep, send = gram([regrouped, swap(regrouped, size, 2)], 1, scale)
    total = keep + swap(send, size, 1)
    terms = [total]
    bit = 4
    while bit < size:
        total = functools.reduce(jnp.add, terms)
        masks = [bit, 2 * bit, 3 * bit] if 2 * bit < size else [bit]
        terms = [total] + [swap(total, size, mask) for mask in masks]
        bit *= 4
    own = factor(terms)
    return apply(own, swap(own, size, 1), held)


def solution(mesh):
    placed = (P("tm", None, "space"), P(), P("tm"))
    return jax.shard_map(
        local, mesh=mesh, in_specs=placed, out_specs=P("tm", None, None, "space"), check_vma=False
    )
```

```python
import functools
import math

import jax
import jax.numpy as jnp
from jax import lax
from jax.experimental import pallas as pl
from jax.experimental.pallas import tpu as pltpu
from jax.sharding import PartitionSpec as P

TILE = 8
CHUNK = 16
VMEM_LIMIT = 48 * 1024 * 1024
PROJECT_VMEM_LIMIT = 60 * 1024 * 1024


def whole_vmem(count):
    return [pl.BlockSpec(memory_space=pltpu.VMEM)] * count


def rows_of(shape):
    return lax.broadcasted_iota(jnp.int32, shape, 0)


def lanes_of(shape):
    return lax.broadcasted_iota(jnp.int32, shape, 1)


def project_kernel(groups, freq_in, offset_in, snap_ref, *refs):
    outs, (freq_ref, offset_ref, held, sems) = refs[:groups], refs[groups:]
    blocks, length, cells = snap_ref.shape
    chunks = blocks // TILE
    small = [
        pltpu.make_async_copy(freq_in, freq_ref, sems.at[chunks]),
        pltpu.make_async_copy(offset_in, offset_ref, sems.at[chunks + 1]),
    ]
    for copy in small:
        copy.start()
    copies = []
    for step in range(chunks):
        part = pl.ds(step * TILE, TILE)
        copies.append(pltpu.make_async_copy(snap_ref.at[part], held.at[part], sems.at[step]))
        copies[-1].start()

    for copy in small:
        copy.wait()
    count = freq_ref.shape[0]
    per_group = count // groups
    first = lax.axis_index("tm") * per_group if groups > 1 else 0
    picked = [freq_ref[lax.rem(first + j, count)] for j in range(count)]

    def turned(moments):
        row = rows_of((2 * count, moments.shape[1]))
        freq = jnp.zeros(row.shape, jnp.int32)
        for j in range(count):
            freq = jnp.where((row == j) | (row == j + count), picked[j], freq)
        turns = lax.rem(freq * moments, length)
        turns = jnp.where(row >= count, turns - length // 4, turns)
        return jnp.cos(turns.astype(jnp.float32) * (2.0 * math.pi / length))

    moments = lanes_of((2 * count, length))
    window = 0.5 - 0.5 * jnp.cos(moments.astype(jnp.float32) * (2.0 * math.pi / length))
    table = window * turned(moments)
    tile_row = rows_of((TILE, length))
    table_rows = []
    for j in range(2 * count):
        spread = jnp.broadcast_to(table[j : j + 1, :], (TILE, length))
        table_rows.append(
            jnp.concatenate([jnp.where(tile_row == b, spread, 0.0) for b in range(TILE)], axis=1)
        )
    spread_table = jnp.concatenate(table_rows, axis=0).astype(jnp.bfloat16)
    phases = turned(jnp.broadcast_to(offset_ref[...], (2 * count, blocks))).T

    for step in range(blocks // CHUNK):
        parts = []
        for half in range(CHUNK // TILE):
            copies[step * (CHUNK // TILE) + half].wait()
            start = step * CHUNK + half * TILE
            data = held[start : start + TILE].reshape(TILE * length, cells)
            projected = jnp.dot(spread_table, data, preferred_element_type=jnp.float32)
            turn = phases[start : start + TILE]
            pairs = []
            for j in range(count):
                cos_part = projected[j * TILE : (j + 1) * TILE]
                sin_part = projected[(count + j) * TILE : (count + j + 1) * TILE]
                cos_phase = turn[:, j : j + 1]
                sin_phase = turn[:, count + j : count + j + 1]
                pairs.append(
                    (
                        cos_part * cos_phase - sin_part * sin_phase,
                        -(sin_part * cos_phase + cos_part * sin_phase),
                    )
                )
            parts.append(pairs)
        for j in range(count):
            for p in range(2):
                value = jnp.concatenate([pairs[j][p] for pairs in parts], axis=0)
                target = outs[j // per_group]
                target[j % per_group, p, step * CHUNK : (step + 1) * CHUNK, :] = value.astype(
                    jnp.bfloat16
                )


def project(snapshots, frequencies, offsets, groups):
    blocks, length, cells = snapshots.shape
    count = frequencies.shape[0]
    shape = jax.ShapeDtypeStruct((count // groups, 2, blocks, cells), jnp.bfloat16)
    return pl.pallas_call(
        functools.partial(project_kernel, groups),
        out_shape=[shape] * groups,
        in_specs=[pl.BlockSpec(memory_space=pltpu.HBM)] * 3,
        out_specs=whole_vmem(groups),
        scratch_shapes=[
            pltpu.SMEM((count,), jnp.int32),
            pltpu.VMEM((1, blocks), jnp.int32),
            pltpu.VMEM(snapshots.shape, snapshots.dtype),
            pltpu.SemaphoreType.DMA((blocks // TILE + 2,)),
        ],
        compiler_params=pltpu.CompilerParams(vmem_limit_bytes=PROJECT_VMEM_LIMIT),
        name="project",
    )(frequencies, offsets.reshape(1, blocks), snapshots)


def gram_kernel(halves, scale, *refs):
    pieces = refs[: 2 * halves]
    held_ref, keep_ref, send_ref, other, packed = refs[2 * halves :]
    count = held_ref.shape[0]
    order = held_ref.shape[2]
    first = lax.axis_index("tm") if halves > 1 else 0
    size = order // halves
    for s, target in ((0, held_ref), (1, other)):
        for h in range(halves):
            place = pl.ds(pl.multiple_of(lax.rem(first + h, halves) * size, size), size)
            target[:, :, place, :] = pieces[s * halves + h][...]
    lower = rows_of((order, order)) >= lanes_of((order, order))
    turn = (((1,), (1,)), ((), ()))
    for f in range(count):
        real = jnp.concatenate([held_ref[f, 0], other[f, 0]], axis=1)
        imag = jnp.concatenate([held_ref[f, 1], other[f, 1]], axis=1)
        both = jnp.concatenate([real, imag], axis=1)
        crossed = jnp.concatenate([imag, -real], axis=1)
        gram_real = lax.dot_general(both, both, turn, preferred_element_type=jnp.float32)
        gram_imag = lax.dot_general(crossed, both, turn, preferred_element_type=jnp.float32)
        packed[f] = jnp.where(lower, gram_real, gram_imag) * scale
    bit = lax.rem(lax.axis_index("space"), 2)
    part = count // 2
    keep_ref[...] = packed[pl.ds(bit * part, part)]
    send_ref[...] = packed[pl.ds((1 - bit) * part, part)]


def gram(pieces, halves, scale):
    count, _, size, cells = pieces[0].shape
    order = size * halves
    held = jax.ShapeDtypeStruct((count, 2, order, cells), jnp.bfloat16)
    half = jax.ShapeDtypeStruct((count // 2, order, order), jnp.float32)
    return pl.pallas_call(
        functools.partial(gram_kernel, halves, scale),
        out_shape=[held, half, half],
        in_specs=whole_vmem(len(pieces)),
        out_specs=whole_vmem(3),
        scratch_shapes=[
            pltpu.VMEM(held.shape, held.dtype),
            pltpu.VMEM((count, order, order), jnp.float32),
        ],
        compiler_params=pltpu.CompilerParams(vmem_limit_bytes=VMEM_LIMIT),
        name="gram",
    )(*pieces)


def spread_row(tile, p):
    return jnp.broadcast_to(tile[p : p + 1, :], tile.shape)


def spread_lane(tile, p):
    return jnp.broadcast_to(tile[:, p : p + 1], tile.shape)


def invert_factor(packed, out_ref, slot):
    order = packed.shape[0]
    shape = (TILE, order)
    tiles = order // TILE
    flipped = packed.T
    row, lane = rows_of((order, order)), lanes_of((order, order))
    full_real = jnp.where(row >= lane, packed, flipped)
    full_imag = jnp.where(row < lane, packed, jnp.where(row == lane, 0.0, -flipped))
    real = [full_real[t * TILE : (t + 1) * TILE] for t in range(tiles)]
    imag = [full_imag[t * TILE : (t + 1) * TILE] for t in range(tiles)]
    tile_row, tile_lane = rows_of(shape), lanes_of(shape)
    at_row = [tile_row == p for p in range(TILE)]
    for k in range(tiles):
        base = k * TILE
        inside = (tile_lane >= base) & (tile_lane < base + TILE)
        col_real = [spread_lane(real[k], base + q) for q in range(TILE)]
        col_imag = [spread_lane(imag[k], base + q) for q in range(TILE)]
        here_real = jnp.where(inside, jnp.where(tile_lane == base + tile_row, 1.0, 0.0), real[k])
        here_imag = jnp.where(inside, 0.0, imag[k])
        done_real, done_imag = here_real, here_imag
        for p in range(TILE):
            pivot = spread_row(col_real[p], p)
            inverse = 1.0 / pivot
            root = lax.rsqrt(pivot)
            done_real = jnp.where(at_row[p], here_real * root, done_real)
            done_imag = jnp.where(at_row[p], here_imag * root, done_imag)
            lead_real, lead_imag = col_real[p], col_imag[p]

            def eliminate(a_real, a_imag):
                top_real = spread_row(a_real, p) * inverse
                top_imag = spread_row(a_imag, p) * inverse
                new_real = a_real - (lead_real * top_real - lead_imag * top_imag)
                new_imag = a_imag - (lead_real * top_imag + lead_imag * top_real)
                return (
                    jnp.where(at_row[p], top_real, new_real),
                    jnp.where(at_row[p], top_imag, new_imag),
                )

            for q in range(p + 1, TILE):
                col_real[q], col_imag[q] = eliminate(col_real[q], col_imag[q])
            here_real, here_imag = eliminate(here_real, here_imag)
        keep = tile_lane < base + TILE
        out_ref[slot, 0, base : base + TILE, :] = jnp.where(keep, done_real, 0.0)
        out_ref[slot, 1, base : base + TILE, :] = jnp.where(keep, done_imag, 0.0)
        if k + 1 < tiles:
            rows_real = [spread_row(here_real, p) for p in range(TILE)]
            rows_imag = [spread_row(here_imag, p) for p in range(TILE)]
        for t in range(k + 1, tiles):
            a_real = jnp.where(inside, 0.0, real[t])
            a_imag = jnp.where(inside, 0.0, imag[t])
            for p in range(TILE):
                lead_real = spread_lane(real[t], base + p)
                lead_imag = spread_lane(imag[t], base + p)
                a_real = a_real - lead_real * rows_real[p] + lead_imag * rows_imag[p]
                a_imag = a_imag - lead_real * rows_imag[p] - lead_imag * rows_real[p]
            real[t], imag[t] = a_real, a_imag


def factor_kernel(terms, *refs):
    out_ref = refs[terms]
    total = refs[0][...]
    for r in refs[1:terms]:
        total = total + r[...]
    for slot in range(total.shape[0]):
        invert_factor(total[slot], out_ref, slot)


def factor(terms):
    count, order, _ = terms[0].shape
    return pl.pallas_call(
        functools.partial(factor_kernel, len(terms)),
        out_shape=jax.ShapeDtypeStruct((count, 2, order, order), jnp.float32),
        in_specs=whole_vmem(len(terms)),
        out_specs=pl.BlockSpec(memory_space=pltpu.VMEM),
        compiler_params=pltpu.CompilerParams(vmem_limit_bytes=VMEM_LIMIT),
        name="factor",
    )(*terms)


def apply_kernel(own_ref, sent_ref, held_ref, out_ref):
    part = own_ref.shape[0]
    order = held_ref.shape[2]
    bit = lax.rem(lax.axis_index("space"), 2)
    for which, source in ((bit, own_ref), (1 - bit, sent_ref)):
        for slot in range(part):
            f = which * part + slot
            real, imag = source[slot, 0], source[slot, 1]
            full = jnp.concatenate(
                [
                    jnp.concatenate([real, -imag], axis=1),
                    jnp.concatenate([imag, real], axis=1),
                ],
                axis=0,
            )
            high = full.astype(jnp.bfloat16)
            low = (full - high.astype(jnp.float32)).astype(jnp.bfloat16)
            data = held_ref[f].reshape(2 * order, held_ref.shape[3])
            value = jnp.dot(high, data, preferred_element_type=jnp.float32) + jnp.dot(
                low, data, preferred_element_type=jnp.float32
            )
            out_ref[f] = value.reshape(held_ref.shape[1:])


def apply(own, sent, held):
    return pl.pallas_call(
        apply_kernel,
        out_shape=jax.ShapeDtypeStruct(held.shape, jnp.float32),
        in_specs=whole_vmem(3),
        out_specs=pl.BlockSpec(memory_space=pltpu.VMEM),
        compiler_params=pltpu.CompilerParams(vmem_limit_bytes=VMEM_LIMIT),
        name="apply",
    )(own, sent, held)


def swap(value, size, mask):
    return lax.ppermute(value, "space", [(i, i ^ mask) for i in range(size)])


def swap_both(value, size, mask):
    pairs = [(t * size + i, (1 - t) * size + (i ^ mask)) for t in range(2) for i in range(size)]
    return lax.ppermute(value, ("tm", "space"), pairs)


def local(snapshots, frequencies, offsets):
    halves = lax.axis_size("tm")
    size = lax.axis_size("space")
    scale = 1.0 / (snapshots.shape[2] * size)
    if halves == 2:
        mine, theirs = project(snapshots, frequencies, offsets, 2)
        pieces = [
            mine,
            swap_both(theirs, size, 0),
            swap(mine, size, 2),
            swap_both(theirs, size, 2),
        ]
        held, keep, send = gram(pieces, 2, scale)
    else:
        (coeffs,) = project(snapshots, frequencies, offsets, 1)
        regrouped = lax.all_to_all(coeffs, "tm", split_axis=0, concat_axis=2, tiled=True)
        held, keep, send = gram([regrouped, swap(regrouped, size, 2)], 1, scale)
    total = keep + swap(send, size, 1)
    terms = [total]
    bit = 4
    while bit < size:
        total = functools.reduce(jnp.add, terms)
        masks = [bit, 2 * bit, 3 * bit] if 2 * bit < size else [bit]
        terms = [total] + [swap(total, size, mask) for mask in masks]
        bit *= 4
    own = factor(terms)
    return apply(own, swap(own, size, 1), held)


def solution(mesh):
    placed = (P("tm", None, "space"), P(), P("tm"))
    return jax.shard_map(
        local, mesh=mesh, in_specs=placed, out_specs=P("tm", None, None, "space"), check_vma=False
    )
```

```python
import functools
import math

import jax
import jax.numpy as jnp
from jax import lax
from jax.experimental import pallas as pl
from jax.experimental.pallas import tpu as pltpu
from jax.sharding import PartitionSpec as P

TILE = 8
CHUNK = 16
VMEM_LIMIT = 32 * 1024 * 1024


def whole_vmem(count):
    return [pl.BlockSpec(memory_space=pltpu.VMEM)] * count


def rows_of(shape):
    return lax.broadcasted_iota(jnp.int32, shape, 0)


def lanes_of(shape):
    return lax.broadcasted_iota(jnp.int32, shape, 1)


def project_kernel(groups, freq_in, offset_in, snap_ref, *refs):
    outs, (freq_ref, offset_ref, held, sems) = refs[:groups], refs[groups:]
    blocks, length, cells = snap_ref.shape
    chunks = blocks // TILE
    small = [
        pltpu.make_async_copy(freq_in, freq_ref, sems.at[chunks]),
        pltpu.make_async_copy(offset_in, offset_ref, sems.at[chunks + 1]),
    ]
    for copy in small:
        copy.start()
    copies = []
    for step in range(chunks):
        part = pl.ds(step * TILE, TILE)
        copies.append(pltpu.make_async_copy(snap_ref.at[part], held.at[part], sems.at[step]))
        copies[-1].start()

    for copy in small:
        copy.wait()
    count = freq_ref.shape[0]
    per_group = count // groups
    first = lax.axis_index("tm") * per_group if groups > 1 else 0
    picked = [freq_ref[lax.rem(first + j, count)] for j in range(count)]

    def turned(moments):
        row = rows_of((2 * count, moments.shape[1]))
        freq = jnp.zeros(row.shape, jnp.int32)
        for j in range(count):
            freq = jnp.where((row == j) | (row == j + count), picked[j], freq)
        turns = lax.rem(freq * moments, length)
        turns = jnp.where(row >= count, turns - length // 4, turns)
        return jnp.cos(turns.astype(jnp.float32) * (2.0 * math.pi / length))

    moments = lanes_of((2 * count, length))
    window = 0.5 - 0.5 * jnp.cos(moments.astype(jnp.float32) * (2.0 * math.pi / length))
    table = window * turned(moments)
    tile_row = rows_of((TILE, length))
    table_rows = []
    for j in range(2 * count):
        spread = jnp.broadcast_to(table[j : j + 1, :], (TILE, length))
        table_rows.append(
            jnp.concatenate([jnp.where(tile_row == b, spread, 0.0) for b in range(TILE)], axis=1)
        )
    spread_table = jnp.concatenate(table_rows, axis=0).astype(jnp.bfloat16)
    phases = turned(jnp.broadcast_to(offset_ref[...], (2 * count, blocks))).T

    for step in range(blocks // CHUNK):
        parts = []
        for half in range(CHUNK // TILE):
            copies[step * (CHUNK // TILE) + half].wait()
            start = step * CHUNK + half * TILE
            data = held[start : start + TILE].reshape(TILE * length, cells)
            projected = jnp.dot(spread_table, data, preferred_element_type=jnp.float32)
            turn = phases[start : start + TILE]
            pairs = []
            for j in range(count):
                cos_part = projected[j * TILE : (j + 1) * TILE]
                sin_part = projected[(count + j) * TILE : (count + j + 1) * TILE]
                cos_phase = turn[:, j : j + 1]
                sin_phase = turn[:, count + j : count + j + 1]
                pairs.append(
                    (
                        cos_part * cos_phase - sin_part * sin_phase,
                        -(sin_part * cos_phase + cos_part * sin_phase),
                    )
                )
            parts.append(pairs)
        for j in range(count):
            for p in range(2):
                value = jnp.concatenate([pairs[j][p] for pairs in parts], axis=0)
                target = outs[j // per_group]
                target[j % per_group, p, step * CHUNK : (step + 1) * CHUNK, :] = value.astype(
                    jnp.bfloat16
                )


def project(snapshots, frequencies, offsets, groups):
    blocks, length, cells = snapshots.shape
    count = frequencies.shape[0]
    shape = pltpu.VMEM((count // groups, 2, blocks, cells), jnp.bfloat16)
    operands = [
        pltpu.with_memory_space_constraint(operand, pltpu.HBM)
        for operand in (frequencies, offsets.reshape(1, blocks), snapshots)
    ]
    return pl.pallas_call(
        functools.partial(project_kernel, groups),
        out_shape=[shape] * groups,
        in_specs=[pl.BlockSpec(memory_space=pltpu.HBM)] * 3,
        out_specs=whole_vmem(groups),
        scratch_shapes=[
            pltpu.SMEM((count,), jnp.int32),
            pltpu.VMEM((1, blocks), jnp.int32),
            pltpu.VMEM(snapshots.shape, snapshots.dtype),
            pltpu.SemaphoreType.DMA((blocks // TILE + 2,)),
        ],
        compiler_params=pltpu.CompilerParams(vmem_limit_bytes=VMEM_LIMIT),
        name="project",
    )(*operands)


def gram_kernel(halves, scale, *refs):
    pieces = refs[: 2 * halves]
    held_ref, keep_ref, send_ref, other, packed = refs[2 * halves :]
    count = held_ref.shape[0]
    order = held_ref.shape[2]
    first = lax.axis_index("tm") if halves > 1 else 0
    size = order // halves
    for s, target in ((0, held_ref), (1, other)):
        for h in range(halves):
            place = pl.ds(pl.multiple_of(lax.rem(first + h, halves) * size, size), size)
            target[:, :, place, :] = pieces[s * halves + h][...]
    lower = rows_of((order, order)) >= lanes_of((order, order))
    turn = (((1,), (1,)), ((), ()))
    for f in range(count):
        real = jnp.concatenate([held_ref[f, 0], other[f, 0]], axis=1)
        imag = jnp.concatenate([held_ref[f, 1], other[f, 1]], axis=1)
        both = jnp.concatenate([real, imag], axis=1)
        crossed = jnp.concatenate([imag, -real], axis=1)
        gram_real = lax.dot_general(both, both, turn, preferred_element_type=jnp.float32)
        gram_imag = lax.dot_general(crossed, both, turn, preferred_element_type=jnp.float32)
        packed[f] = jnp.where(lower, gram_real, gram_imag) * scale
    bit = lax.rem(lax.axis_index("space"), 2)
    part = count // 2
    keep_ref[...] = packed[pl.ds(bit * part, part)]
    send_ref[...] = packed[pl.ds((1 - bit) * part, part)]


def gram(pieces, halves, scale):
    count, _, size, cells = pieces[0].shape
    order = size * halves
    held = jax.ShapeDtypeStruct((count, 2, order, cells), jnp.bfloat16)
    half = jax.ShapeDtypeStruct((count // 2, order, order), jnp.float32)
    return pl.pallas_call(
        functools.partial(gram_kernel, halves, scale),
        out_shape=[held, half, half],
        in_specs=whole_vmem(len(pieces)),
        out_specs=whole_vmem(3),
        scratch_shapes=[
            pltpu.VMEM(held.shape, held.dtype),
            pltpu.VMEM((count, order, order), jnp.float32),
        ],
        compiler_params=pltpu.CompilerParams(vmem_limit_bytes=VMEM_LIMIT),
        name="gram",
    )(*pieces)


def spread_row(tile, p):
    return jnp.broadcast_to(tile[p : p + 1, :], tile.shape)


def spread_lane(tile, p):
    return jnp.broadcast_to(tile[:, p : p + 1], tile.shape)


def invert_factor(packed, out_ref, slot):
    order = packed.shape[0]
    shape = (TILE, order)
    tiles = order // TILE
    flipped = packed.T
    row, lane = rows_of((order, order)), lanes_of((order, order))
    full_real = jnp.where(row >= lane, packed, flipped)
    full_imag = jnp.where(row < lane, packed, jnp.where(row == lane, 0.0, -flipped))
    real = [full_real[t * TILE : (t + 1) * TILE] for t in range(tiles)]
    imag = [full_imag[t * TILE : (t + 1) * TILE] for t in range(tiles)]
    tile_row, tile_lane = rows_of(shape), lanes_of(shape)
    at_row = [tile_row == p for p in range(TILE)]
    for k in range(tiles):
        base = k * TILE
        inside = (tile_lane >= base) & (tile_lane < base + TILE)
        col_real = [spread_lane(real[k], base + q) for q in range(TILE)]
        col_imag = [spread_lane(imag[k], base + q) for q in range(TILE)]
        here_real = jnp.where(inside, jnp.where(tile_lane == base + tile_row, 1.0, 0.0), real[k])
        here_imag = jnp.where(inside, 0.0, imag[k])
        done_real, done_imag = here_real, here_imag
        for p in range(TILE):
            pivot = spread_row(col_real[p], p)
            inverse = 1.0 / pivot
            root = lax.rsqrt(pivot)
            done_real = jnp.where(at_row[p], here_real * root, done_real)
            done_imag = jnp.where(at_row[p], here_imag * root, done_imag)
            lead_real, lead_imag = col_real[p], col_imag[p]

            def eliminate(a_real, a_imag):
                top_real = spread_row(a_real, p) * inverse
                top_imag = spread_row(a_imag, p) * inverse
                new_real = a_real - (lead_real * top_real - lead_imag * top_imag)
                new_imag = a_imag - (lead_real * top_imag + lead_imag * top_real)
                return (
                    jnp.where(at_row[p], top_real, new_real),
                    jnp.where(at_row[p], top_imag, new_imag),
                )

            for q in range(p + 1, TILE):
                col_real[q], col_imag[q] = eliminate(col_real[q], col_imag[q])
            here_real, here_imag = eliminate(here_real, here_imag)
        keep = tile_lane < base + TILE
        out_ref[slot, 0, base : base + TILE, :] = jnp.where(keep, done_real, 0.0)
        out_ref[slot, 1, base : base + TILE, :] = jnp.where(keep, done_imag, 0.0)
        if k + 1 < tiles:
            rows_real = [spread_row(here_real, p) for p in range(TILE)]
            rows_imag = [spread_row(here_imag, p) for p in range(TILE)]
        for t in range(k + 1, tiles):
            a_real = jnp.where(inside, 0.0, real[t])
            a_imag = jnp.where(inside, 0.0, imag[t])
            for p in range(TILE):
                lead_real = spread_lane(real[t], base + p)
                lead_imag = spread_lane(imag[t], base + p)
                a_real = a_real - lead_real * rows_real[p] + lead_imag * rows_imag[p]
                a_imag = a_imag - lead_real * rows_imag[p] - lead_imag * rows_real[p]
            real[t], imag[t] = a_real, a_imag


def factor_kernel(terms, *refs):
    out_ref = refs[terms]
    total = refs[0][...]
    for r in refs[1:terms]:
        total = total + r[...]
    for slot in range(total.shape[0]):
        invert_factor(total[slot], out_ref, slot)


def factor(terms):
    count, order, _ = terms[0].shape
    return pl.pallas_call(
        functools.partial(factor_kernel, len(terms)),
        out_shape=jax.ShapeDtypeStruct((count, 2, order, order), jnp.float32),
        in_specs=whole_vmem(len(terms)),
        out_specs=pl.BlockSpec(memory_space=pltpu.VMEM),
        compiler_params=pltpu.CompilerParams(vmem_limit_bytes=VMEM_LIMIT),
        name="factor",
    )(*terms)


def apply_kernel(own_ref, sent_ref, held_ref, out_ref):
    part = own_ref.shape[0]
    order = held_ref.shape[2]
    bit = lax.rem(lax.axis_index("space"), 2)
    for which, source in ((bit, own_ref), (1 - bit, sent_ref)):
        for slot in range(part):
            f = which * part + slot
            real, imag = source[slot, 0], source[slot, 1]
            full = jnp.concatenate(
                [
                    jnp.concatenate([real, -imag], axis=1),
                    jnp.concatenate([imag, real], axis=1),
                ],
                axis=0,
            )
            high = full.astype(jnp.bfloat16)
            low = (full - high.astype(jnp.float32)).astype(jnp.bfloat16)
            data = held_ref[f].reshape(2 * order, held_ref.shape[3])
            value = jnp.dot(high, data, preferred_element_type=jnp.float32) + jnp.dot(
                low, data, preferred_element_type=jnp.float32
            )
            out_ref[f] = value.reshape(held_ref.shape[1:])


def apply(own, sent, held):
    return pl.pallas_call(
        apply_kernel,
        out_shape=jax.ShapeDtypeStruct(held.shape, jnp.float32),
        in_specs=whole_vmem(3),
        out_specs=pl.BlockSpec(memory_space=pltpu.VMEM),
        compiler_params=pltpu.CompilerParams(vmem_limit_bytes=VMEM_LIMIT),
        name="apply",
    )(own, sent, held)


def swap(value, size, mask):
    return lax.ppermute(value, "space", [(i, i ^ mask) for i in range(size)])


def swap_both(value, size, mask):
    pairs = [(t * size + i, (1 - t) * size + (i ^ mask)) for t in range(2) for i in range(size)]
    return lax.ppermute(value, ("tm", "space"), pairs)


def local(snapshots, frequencies, offsets):
    halves = lax.axis_size("tm")
    size = lax.axis_size("space")
    scale = 1.0 / (snapshots.shape[2] * size)
    if halves == 2:
        mine, theirs = project(snapshots, frequencies, offsets, 2)
        pieces = [
            mine,
            swap_both(theirs, size, 0),
            swap(mine, size, 2),
            swap_both(theirs, size, 2),
        ]
        held, keep, send = gram(pieces, 2, scale)
    else:
        (coeffs,) = project(snapshots, frequencies, offsets, 1)
        regrouped = lax.all_to_all(coeffs, "tm", split_axis=0, concat_axis=2, tiled=True)
        held, keep, send = gram([regrouped, swap(regrouped, size, 2)], 1, scale)
    total = keep + swap(send, size, 1)
    terms = [total]
    bit = 4
    while bit < size:
        total = functools.reduce(jnp.add, terms)
        masks = [bit, 2 * bit, 3 * bit] if 2 * bit < size else [bit]
        terms = [total] + [swap(total, size, mask) for mask in masks]
        bit *= 4
    own = factor(terms)
    return apply(own, swap(own, size, 1), held)


def solution(mesh):
    placed = (P("tm", None, "space"), P(), P("tm"))
    return jax.shard_map(
        local, mesh=mesh, in_specs=placed, out_specs=P("tm", None, None, "space"), check_vma=False
    )
```

```python
import functools
import math

import jax
import jax.numpy as jnp
from jax import lax
from jax.experimental import pallas as pl
from jax.experimental.pallas import tpu as pltpu
from jax.sharding import PartitionSpec as P

TILE = 8
CHUNK = 16
VMEM_LIMIT = 32 * 1024 * 1024


def whole_vmem(count):
    return [pl.BlockSpec(memory_space=pltpu.VMEM)] * count


def rows_of(shape):
    return lax.broadcasted_iota(jnp.int32, shape, 0)


def lanes_of(shape):
    return lax.broadcasted_iota(jnp.int32, shape, 1)


def project_kernel(groups, freq_in, offset_in, snap_ref, *refs):
    outs, (freq_ref, offset_ref, held, sems) = refs[:groups], refs[groups:]
    blocks, length, cells = snap_ref.shape
    chunks = blocks // TILE
    small = [
        pltpu.make_async_copy(freq_in, freq_ref, sems.at[chunks]),
        pltpu.make_async_copy(offset_in, offset_ref, sems.at[chunks + 1]),
    ]
    for copy in small:
        copy.start()
    copies = []
    for step in range(chunks):
        part = pl.ds(step * TILE, TILE)
        copies.append(pltpu.make_async_copy(snap_ref.at[part], held.at[part], sems.at[step]))
        copies[-1].start()

    for copy in small:
        copy.wait()
    count = freq_ref.shape[0]
    per_group = count // groups
    first = lax.axis_index("tm") * per_group if groups > 1 else 0
    picked = [freq_ref[lax.rem(first + j, count)] for j in range(count)]

    def turned(moments):
        row = rows_of((2 * count, moments.shape[1]))
        freq = jnp.zeros(row.shape, jnp.int32)
        for j in range(count):
            freq = jnp.where((row == j) | (row == j + count), picked[j], freq)
        turns = lax.rem(freq * moments, length)
        turns = jnp.where(row >= count, turns - length // 4, turns)
        return jnp.cos(turns.astype(jnp.float32) * (2.0 * math.pi / length))

    moments = lanes_of((2 * count, length))
    window = 0.5 - 0.5 * jnp.cos(moments.astype(jnp.float32) * (2.0 * math.pi / length))
    table = window * turned(moments)
    tile_row = rows_of((TILE, length))
    table_rows = []
    for j in range(2 * count):
        spread = jnp.broadcast_to(table[j : j + 1, :], (TILE, length))
        table_rows.append(
            jnp.concatenate([jnp.where(tile_row == b, spread, 0.0) for b in range(TILE)], axis=1)
        )
    spread_table = jnp.concatenate(table_rows, axis=0).astype(jnp.bfloat16)
    phases = turned(jnp.broadcast_to(offset_ref[...], (2 * count, blocks))).T

    for step in range(blocks // CHUNK):
        parts = []
        for half in range(CHUNK // TILE):
            copies[step * (CHUNK // TILE) + half].wait()
        for half in range(CHUNK // TILE):
            start = step * CHUNK + half * TILE
            data = held[start : start + TILE].reshape(TILE * length, cells)
            projected = jnp.dot(spread_table, data, preferred_element_type=jnp.float32)
            turn = phases[start : start + TILE]
            pairs = []
            for j in range(count):
                cos_part = projected[j * TILE : (j + 1) * TILE]
                sin_part = projected[(count + j) * TILE : (count + j + 1) * TILE]
                cos_phase = turn[:, j : j + 1]
                sin_phase = turn[:, count + j : count + j + 1]
                pairs.append(
                    (
                        cos_part * cos_phase - sin_part * sin_phase,
                        -(sin_part * cos_phase + cos_part * sin_phase),
                    )
                )
            parts.append(pairs)
        for j in range(count):
            for p in range(2):
                value = jnp.concatenate([pairs[j][p] for pairs in parts], axis=0)
                target = outs[j // per_group]
                target[j % per_group, p, step * CHUNK : (step + 1) * CHUNK, :] = value.astype(
                    jnp.bfloat16
                )


def project(snapshots, frequencies, offsets, groups):
    blocks, length, cells = snapshots.shape
    count = frequencies.shape[0]
    shape = pltpu.VMEM((count // groups, 2, blocks, cells), jnp.bfloat16)
    operands = [
        pltpu.with_memory_space_constraint(operand, pltpu.HBM)
        for operand in (frequencies, offsets.reshape(1, blocks), snapshots)
    ]
    return pl.pallas_call(
        functools.partial(project_kernel, groups),
        out_shape=[shape] * groups,
        in_specs=[pl.BlockSpec(memory_space=pltpu.HBM)] * 3,
        out_specs=whole_vmem(groups),
        scratch_shapes=[
            pltpu.SMEM((count,), jnp.int32),
            pltpu.VMEM((1, blocks), jnp.int32),
            pltpu.VMEM(snapshots.shape, snapshots.dtype),
            pltpu.SemaphoreType.DMA((blocks // TILE + 2,)),
        ],
        compiler_params=pltpu.CompilerParams(vmem_limit_bytes=VMEM_LIMIT),
        name="project",
    )(*operands)


def gram_kernel(halves, scale, *refs):
    pieces = refs[:halves]
    held_ref, keep_ref, send_ref, packed = refs[halves:]
    count = held_ref.shape[0]
    order = held_ref.shape[2]
    first = lax.axis_index("tm") if halves > 1 else 0
    size = order // halves
    for h in range(halves):
        place = pl.ds(pl.multiple_of(lax.rem(first + h, halves) * size, size), size)
        held_ref[:, :, place, :] = pieces[h][...]
    lower = rows_of((order, order)) >= lanes_of((order, order))
    turn = (((1,), (1,)), ((), ()))
    for f in range(count):
        real, imag = held_ref[f, 0], held_ref[f, 1]
        both = jnp.concatenate([real, imag], axis=1)
        crossed = jnp.concatenate([imag, -real], axis=1)
        gram_real = lax.dot_general(both, both, turn, preferred_element_type=jnp.float32)
        gram_imag = lax.dot_general(crossed, both, turn, preferred_element_type=jnp.float32)
        packed[f] = jnp.where(lower, gram_real, gram_imag) * scale
    bit = lax.rem(lax.axis_index("space"), 2)
    part = count // 2
    keep_ref[...] = packed[pl.ds(bit * part, part)]
    send_ref[...] = packed[pl.ds((1 - bit) * part, part)]


def gram(pieces, halves, scale):
    count, _, size, cells = pieces[0].shape
    order = size * halves
    held = jax.ShapeDtypeStruct((count, 2, order, cells), jnp.bfloat16)
    half = jax.ShapeDtypeStruct((count // 2, order, order), jnp.float32)
    return pl.pallas_call(
        functools.partial(gram_kernel, halves, scale),
        out_shape=[held, half, half],
        in_specs=whole_vmem(len(pieces)),
        out_specs=whole_vmem(3),
        scratch_shapes=[
            pltpu.VMEM((count, order, order), jnp.float32),
        ],
        compiler_params=pltpu.CompilerParams(vmem_limit_bytes=VMEM_LIMIT),
        name="gram",
    )(*pieces)


def spread_row(tile, p):
    return jnp.broadcast_to(tile[p : p + 1, :], tile.shape)


def spread_lane(tile, p):
    return jnp.broadcast_to(tile[:, p : p + 1], tile.shape)


def invert_factor(packed, out_ref, slot):
    order = packed.shape[0]
    shape = (TILE, order)
    tiles = order // TILE
    flipped = packed.T
    row, lane = rows_of((order, order)), lanes_of((order, order))
    full_real = jnp.where(row >= lane, packed, flipped)
    full_imag = jnp.where(row < lane, packed, jnp.where(row == lane, 0.0, -flipped))
    real = [full_real[t * TILE : (t + 1) * TILE] for t in range(tiles)]
    imag = [full_imag[t * TILE : (t + 1) * TILE] for t in range(tiles)]
    tile_row, tile_lane = rows_of(shape), lanes_of(shape)
    at_row = [tile_row == p for p in range(TILE)]
    for k in range(tiles):
        base = k * TILE
        inside = (tile_lane >= base) & (tile_lane < base + TILE)
        col_real = [spread_lane(real[k], base + q) for q in range(TILE)]
        col_imag = [spread_lane(imag[k], base + q) for q in range(TILE)]
        here_real = jnp.where(inside, jnp.where(tile_lane == base + tile_row, 1.0, 0.0), real[k])
        here_imag = jnp.where(inside, 0.0, imag[k])
        done_real, done_imag = here_real, here_imag
        for p in range(TILE):
            pivot = spread_row(col_real[p], p)
            inverse = 1.0 / pivot
            root = lax.rsqrt(pivot)
            done_real = jnp.where(at_row[p], here_real * root, done_real)
            done_imag = jnp.where(at_row[p], here_imag * root, done_imag)
            lead_real, lead_imag = col_real[p], col_imag[p]

            def eliminate(a_real, a_imag):
                top_real = spread_row(a_real, p) * inverse
                top_imag = spread_row(a_imag, p) * inverse
                new_real = a_real - (lead_real * top_real - lead_imag * top_imag)
                new_imag = a_imag - (lead_real * top_imag + lead_imag * top_real)
                return (
                    jnp.where(at_row[p], top_real, new_real),
                    jnp.where(at_row[p], top_imag, new_imag),
                )

            for q in range(p + 1, TILE):
                col_real[q], col_imag[q] = eliminate(col_real[q], col_imag[q])
            here_real, here_imag = eliminate(here_real, here_imag)
        keep = tile_lane < base + TILE
        out_ref[slot, 0, base : base + TILE, :] = jnp.where(keep, done_real, 0.0)
        out_ref[slot, 1, base : base + TILE, :] = jnp.where(keep, done_imag, 0.0)
        if k + 1 < tiles:
            rows_real = [spread_row(here_real, p) for p in range(TILE)]
            rows_imag = [spread_row(here_imag, p) for p in range(TILE)]
        for t in range(k + 1, tiles):
            a_real = jnp.where(inside, 0.0, real[t])
            a_imag = jnp.where(inside, 0.0, imag[t])
            for p in range(TILE):
                lead_real = spread_lane(real[t], base + p)
                lead_imag = spread_lane(imag[t], base + p)
                a_real = a_real - lead_real * rows_real[p] + lead_imag * rows_imag[p]
                a_imag = a_imag - lead_real * rows_imag[p] - lead_imag * rows_real[p]
            real[t], imag[t] = a_real, a_imag


def factor_kernel(terms, *refs):
    out_ref = refs[terms]
    total = refs[0][...]
    for r in refs[1:terms]:
        total = total + r[...]
    for slot in range(total.shape[0]):
        invert_factor(total[slot], out_ref, slot)


def factor(terms):
    count, order, _ = terms[0].shape
    return pl.pallas_call(
        functools.partial(factor_kernel, len(terms)),
        out_shape=jax.ShapeDtypeStruct((count, 2, order, order), jnp.float32),
        in_specs=whole_vmem(len(terms)),
        out_specs=pl.BlockSpec(memory_space=pltpu.VMEM),
        compiler_params=pltpu.CompilerParams(vmem_limit_bytes=VMEM_LIMIT),
        name="factor",
    )(*terms)


def apply_kernel(own_ref, sent_ref, held_ref, out_ref):
    part = own_ref.shape[0]
    order = held_ref.shape[2]
    bit = lax.rem(lax.axis_index("space"), 2)
    for which, source in ((bit, own_ref), (1 - bit, sent_ref)):
        for slot in range(part):
            f = which * part + slot
            real, imag = source[slot, 0], source[slot, 1]
            full = jnp.concatenate(
                [
                    jnp.concatenate([real, -imag], axis=1),
                    jnp.concatenate([imag, real], axis=1),
                ],
                axis=0,
            )
            high = full.astype(jnp.bfloat16)
            low = (full - high.astype(jnp.float32)).astype(jnp.bfloat16)
            data = held_ref[f].reshape(2 * order, held_ref.shape[3])
            value = jnp.dot(high, data, preferred_element_type=jnp.float32) + jnp.dot(
                low, data, preferred_element_type=jnp.float32
            )
            out_ref[f] = value.reshape(held_ref.shape[1:])


def apply(own, sent, held):
    return pl.pallas_call(
        apply_kernel,
        out_shape=jax.ShapeDtypeStruct(held.shape, jnp.float32),
        in_specs=whole_vmem(3),
        out_specs=pl.BlockSpec(memory_space=pltpu.VMEM),
        compiler_params=pltpu.CompilerParams(vmem_limit_bytes=VMEM_LIMIT),
        name="apply",
    )(own, sent, held)


def swap(value, size, mask):
    return lax.ppermute(value, "space", [(i, i ^ mask) for i in range(size)])


def local(snapshots, frequencies, offsets):
    halves = lax.axis_size("tm")
    size = lax.axis_size("space")
    scale = 1.0 / (snapshots.shape[2] * size)
    if halves == 2:
        mine, theirs = project(snapshots, frequencies, offsets, 2)
        pieces = [mine, lax.ppermute(theirs, "tm", [(0, 1), (1, 0)])]
        held, keep, send = gram(pieces, 2, scale)
    else:
        (coeffs,) = project(snapshots, frequencies, offsets, 1)
        regrouped = lax.all_to_all(coeffs, "tm", split_axis=0, concat_axis=2, tiled=True)
        held, keep, send = gram([regrouped], 1, scale)
    total = keep + swap(send, size, 1)
    terms = [total]
    bit = 2
    while bit < size:
        total = functools.reduce(jnp.add, terms)
        masks = [bit, 2 * bit, 3 * bit] if 2 * bit < size else [bit]
        terms = [total] + [swap(total, size, mask) for mask in masks]
        bit *= 4
    own = factor(terms)
    return apply(own, swap(own, size, 1), held)


def solution(mesh):
    placed = (P("tm", None, "space"), P(), P("tm"))
    return jax.shard_map(
        local, mesh=mesh, in_specs=placed, out_specs=P("tm", None, None, "space"), check_vma=False
    )
```

```python
import functools
import math

import jax
import jax.numpy as jnp
from jax import lax
from jax.experimental import pallas as pl
from jax.experimental.pallas import tpu as pltpu
from jax.sharding import PartitionSpec as P

TILE = 8
CHUNK = 16
VMEM_LIMIT = 32 * 1024 * 1024


def whole_vmem(count):
    return [pl.BlockSpec(memory_space=pltpu.VMEM)] * count


def rows_of(shape):
    return lax.broadcasted_iota(jnp.int32, shape, 0)


def lanes_of(shape):
    return lax.broadcasted_iota(jnp.int32, shape, 1)


def project_kernel(groups, freq_in, offset_in, snap_ref, *refs):
    outs, (freq_ref, offset_ref, held, sems) = refs[:groups], refs[groups:]
    blocks, length, cells = snap_ref.shape
    chunks = blocks // TILE
    small = [
        pltpu.make_async_copy(freq_in, freq_ref, sems.at[chunks]),
        pltpu.make_async_copy(offset_in, offset_ref, sems.at[chunks + 1]),
    ]
    for copy in small:
        copy.start()
    copies = []
    for step in range(chunks):
        part = pl.ds(step * TILE, TILE)
        copies.append(pltpu.make_async_copy(snap_ref.at[part], held.at[part], sems.at[step]))
        copies[-1].start()

    for copy in small:
        copy.wait()
    count = freq_ref.shape[0]
    per_group = count // groups
    first = lax.axis_index("tm") * per_group if groups > 1 else 0
    picked = [freq_ref[lax.rem(first + j, count)] for j in range(count)]

    def turned(moments):
        row = rows_of((2 * count, moments.shape[1]))
        freq = jnp.zeros(row.shape, jnp.int32)
        for j in range(count):
            freq = jnp.where((row == j) | (row == j + count), picked[j], freq)
        turns = lax.rem(freq * moments, length)
        turns = jnp.where(row >= count, turns - length // 4, turns)
        return jnp.cos(turns.astype(jnp.float32) * (2.0 * math.pi / length))

    moments = lanes_of((2 * count, length))
    window = 0.5 - 0.5 * jnp.cos(moments.astype(jnp.float32) * (2.0 * math.pi / length))
    table = window * turned(moments)
    tile_row = rows_of((TILE, length))
    table_rows = []
    for j in range(2 * count):
        spread = jnp.broadcast_to(table[j : j + 1, :], (TILE, length))
        table_rows.append(
            jnp.concatenate([jnp.where(tile_row == b, spread, 0.0) for b in range(TILE)], axis=1)
        )
    spread_table = jnp.concatenate(table_rows, axis=0).astype(jnp.bfloat16)
    phases = turned(jnp.broadcast_to(offset_ref[...], (2 * count, blocks))).T

    for step in range(blocks // CHUNK):
        parts = []
        for half in range(CHUNK // TILE):
            copies[step * (CHUNK // TILE) + half].wait()
        for half in range(CHUNK // TILE):
            start = step * CHUNK + half * TILE
            data = held[start : start + TILE].reshape(TILE * length, cells)
            projected = jnp.dot(spread_table, data, preferred_element_type=jnp.float32)
            turn = phases[start : start + TILE]
            pairs = []
            for j in range(count):
                cos_part = projected[j * TILE : (j + 1) * TILE]
                sin_part = projected[(count + j) * TILE : (count + j + 1) * TILE]
                cos_phase = turn[:, j : j + 1]
                sin_phase = turn[:, count + j : count + j + 1]
                pairs.append(
                    (
                        cos_part * cos_phase - sin_part * sin_phase,
                        -(sin_part * cos_phase + cos_part * sin_phase),
                    )
                )
            parts.append(pairs)
        for j in range(count):
            for p in range(2):
                value = jnp.concatenate([pairs[j][p] for pairs in parts], axis=0)
                target = outs[j // per_group]
                target[j % per_group, p, step * CHUNK : (step + 1) * CHUNK, :] = value.astype(
                    jnp.bfloat16
                )


def project(snapshots, frequencies, offsets, groups):
    blocks, length, cells = snapshots.shape
    count = frequencies.shape[0]
    shape = pltpu.VMEM((count // groups, 2, blocks, cells), jnp.bfloat16)
    operands = [
        pltpu.with_memory_space_constraint(operand, pltpu.HBM)
        for operand in (frequencies, offsets.reshape(1, blocks), snapshots)
    ]
    return pl.pallas_call(
        functools.partial(project_kernel, groups),
        out_shape=[shape] * groups,
        in_specs=[pl.BlockSpec(memory_space=pltpu.HBM)] * 3,
        out_specs=whole_vmem(groups),
        scratch_shapes=[
            pltpu.SMEM((count,), jnp.int32),
            pltpu.VMEM((1, blocks), jnp.int32),
            pltpu.VMEM(snapshots.shape, snapshots.dtype),
            pltpu.SemaphoreType.DMA((blocks // TILE + 2,)),
        ],
        compiler_params=pltpu.CompilerParams(vmem_limit_bytes=VMEM_LIMIT),
        name="project",
    )(*operands)


def gram_kernel(halves, scale, *refs):
    pieces = refs[:halves]
    held_ref, keep_ref, send_ref, packed = refs[halves:]
    count = held_ref.shape[0]
    order = held_ref.shape[2]
    first = lax.axis_index("tm") if halves > 1 else 0
    size = order // halves
    for h in range(halves):
        place = pl.ds(pl.multiple_of(lax.rem(first + h, halves) * size, size), size)
        held_ref[:, :, place, :] = pieces[h][...]
    lower = rows_of((order, order)) >= lanes_of((order, order))
    turn = (((1,), (1,)), ((), ()))
    for f in range(count):
        real, imag = held_ref[f, 0], held_ref[f, 1]
        both = jnp.concatenate([real, imag], axis=1)
        crossed = jnp.concatenate([imag, -real], axis=1)
        gram_real = lax.dot_general(both, both, turn, preferred_element_type=jnp.float32)
        gram_imag = lax.dot_general(crossed, both, turn, preferred_element_type=jnp.float32)
        packed[f] = jnp.where(lower, gram_real, gram_imag) * scale
    bit = lax.rem(lax.axis_index("space"), 2)
    part = count // 2
    keep_ref[...] = packed[pl.ds(bit * part, part)]
    send_ref[...] = packed[pl.ds((1 - bit) * part, part)]


def gram(pieces, halves, scale):
    count, _, size, cells = pieces[0].shape
    order = size * halves
    held = jax.ShapeDtypeStruct((count, 2, order, cells), jnp.bfloat16)
    half = jax.ShapeDtypeStruct((count // 2, order, order), jnp.float32)
    return pl.pallas_call(
        functools.partial(gram_kernel, halves, scale),
        out_shape=[held, half, half],
        in_specs=whole_vmem(len(pieces)),
        out_specs=whole_vmem(3),
        scratch_shapes=[
            pltpu.VMEM((count, order, order), jnp.float32),
        ],
        compiler_params=pltpu.CompilerParams(vmem_limit_bytes=VMEM_LIMIT),
        name="gram",
    )(*pieces)


def spread_row(tile, p):
    return jnp.broadcast_to(tile[p : p + 1, :], tile.shape)


def spread_lane(tile, p):
    return jnp.take_along_axis(tile, jnp.full(tile.shape, p, jnp.int32), axis=1)


def add_up(terms):
    while len(terms) > 1:
        pairs = [a + b for a, b in zip(terms[::2], terms[1::2])]
        terms = pairs + terms[len(pairs) * 2 :]
    return terms[0]


def column_pairs(tile, base):
    return [tuple(spread_lane(part, base + p) for part in tile) for p in range(TILE)]


def row_pairs(tile):
    return [tuple(spread_row(part, p) for part in tile) for p in range(TILE)]


def subtract_product(tile, columns, rows):
    pairs = list(zip(columns, rows))
    return (
        tile[0] - add_up([cr * rr - ci * ri for (cr, ci), (rr, ri) in pairs]),
        tile[1] - add_up([cr * ri + ci * rr for (cr, ci), (rr, ri) in pairs]),
    )


def clear_lanes(tile, low, high):
    lane = lanes_of(tile[0].shape)
    cleared = (lane >= low) & (lane < high)
    return tuple(jnp.where(cleared, 0.0, part) for part in tile)


def eliminate_tile(tile, base):
    shape = tile[0].shape
    row = rows_of(shape)
    columns = column_pairs(tile, base)
    real, imag = clear_lanes(tile, base, base + TILE)
    real = jnp.where(lanes_of(shape) == base + row, 1.0, real)
    done_real, done_imag = real, imag
    inverses = jnp.ones(shape, jnp.float32)
    for p in range(TILE):
        here = row == p
        pivot = spread_row(columns[p][0], p)
        inverse = 1.0 / pivot
        root = lax.rsqrt(pivot)
        done_real = jnp.where(here, real * root, done_real)
        done_imag = jnp.where(here, imag * root, done_imag)
        inverses = jnp.where(here, inverse, inverses)
        lead_real, lead_imag = (jnp.where(here, 0.0, part) * inverse for part in columns[p])

        def reduce_rows(a_real, a_imag):
            top_real, top_imag = spread_row(a_real, p), spread_row(a_imag, p)
            return (
                a_real - (lead_real * top_real - lead_imag * top_imag),
                a_imag - (lead_real * top_imag + lead_imag * top_real),
            )

        for q in range(p + 1, TILE):
            columns[q] = reduce_rows(*columns[q])
        real, imag = reduce_rows(real, imag)
    return (done_real, done_imag), (real * inverses, imag * inverses)


def three_parts(value):
    parts = []
    for _ in range(3):
        parts.append(value.astype(jnp.bfloat16))
        value = value - parts[-1].astype(jnp.float32)
    return parts


def outer_product(real, imag):
    reals, imags = three_parts(real), three_parts(imag)
    left = [jnp.concatenate(pair, axis=0) for pair in zip(reals, imags)]
    right = [
        jnp.concatenate(
            [jnp.concatenate([a, b], axis=1), jnp.concatenate([b, -a], axis=1)], axis=0
        )
        for a, b in zip(reals, imags)
    ]
    chosen = [(0, 0), (0, 1), (1, 0), (0, 2), (2, 0), (1, 1)]
    return lax.dot_general(
        jnp.concatenate([left[a] for a, _ in chosen], axis=0),
        jnp.concatenate([right[b] for _, b in chosen], axis=0),
        (((0,), (0,)), ((), ())),
        preferred_element_type=jnp.float32,
    )


def invert_factor(packed, out_ref, slot):
    order = packed.shape[0]
    count = order // TILE
    flipped = packed.T
    row, lane = rows_of((order, order)), lanes_of((order, order))
    full_real = jnp.where(row >= lane, packed, flipped)
    full_imag = jnp.where(row < lane, packed, jnp.where(row == lane, 0.0, -flipped))
    tiles = [
        (full_real[t * TILE : (t + 1) * TILE], full_imag[t * TILE : (t + 1) * TILE])
        for t in range(count)
    ]

    def store(done, base):
        kept = clear_lanes(done, base + TILE, order)
        out_ref[slot, 0, base : base + TILE, :] = kept[0]
        out_ref[slot, 1, base : base + TILE, :] = kept[1]

    for first in range(0, count, 2):
        second = first + 1
        base, middle, end = first * TILE, second * TILE, (second + 1) * TILE
        near = [t for t in (first + 2, first + 3) if t < count]
        columns = column_pairs(tiles[second], base)
        upper_done, upper = eliminate_tile(tiles[first], base)
        store(upper_done, base)
        tiles[second] = subtract_product(
            clear_lanes(tiles[second], base, middle), columns, row_pairs(upper)
        )
        back = column_pairs(upper, middle)
        near_columns = [
            column_pairs(tiles[t], base) + column_pairs(tiles[t], middle) for t in near
        ]
        lower_done, lower = eliminate_tile(tiles[second], middle)
        store(lower_done, middle)
        if not near:
            break
        lower_rows = row_pairs(lower)
        upper = subtract_product(clear_lanes(upper, middle, end), back, lower_rows)
        both_rows = row_pairs(upper) + lower_rows
        for t, lead in zip(near, near_columns):
            tiles[t] = subtract_product(clear_lanes(tiles[t], base, end), lead, both_rows)
        if first + 4 < count:
            upper_done = clear_lanes(upper_done, middle, end)
            change = outer_product(
                *(jnp.concatenate(pair, axis=0) for pair in zip(upper_done, lower_done))
            )
            for t in range(first + 4, count):
                real, imag = clear_lanes(tiles[t], base, end)
                part = change[t * TILE : (t + 1) * TILE]
                tiles[t] = (real - part[:, :order], imag - part[:, order:])


def factor_kernel(terms, *refs):
    out_ref = refs[terms]
    total = refs[0][...]
    for r in refs[1:terms]:
        total = total + r[...]
    for slot in range(total.shape[0]):
        invert_factor(total[slot], out_ref, slot)


def factor(terms):
    count, order, _ = terms[0].shape
    return pl.pallas_call(
        functools.partial(factor_kernel, len(terms)),
        out_shape=jax.ShapeDtypeStruct((count, 2, order, order), jnp.float32),
        in_specs=whole_vmem(len(terms)),
        out_specs=pl.BlockSpec(memory_space=pltpu.VMEM),
        compiler_params=pltpu.CompilerParams(vmem_limit_bytes=VMEM_LIMIT),
        name="factor",
    )(*terms)


def apply_kernel(other, factor_ref, held_ref, *refs):
    out_ref, value_ref, sems = refs[-3:]
    part = factor_ref.shape[0]
    bit = lax.rem(lax.axis_index("space"), 2)
    which = 1 - bit if other else bit
    copies = []
    for slot in range(part):
        f = which * part + slot
        real, imag = factor_ref[slot, 0], factor_ref[slot, 1]
        data = held_ref[f].reshape(2 * held_ref.shape[2], held_ref.shape[3])
        for p, full in enumerate(
            (jnp.concatenate([real, -imag], axis=1), jnp.concatenate([imag, real], axis=1))
        ):
            high = full.astype(jnp.bfloat16)
            low = (full - high.astype(jnp.float32)).astype(jnp.bfloat16)
            value_ref[slot, p] = jnp.dot(high, data, preferred_element_type=jnp.float32) + jnp.dot(
                low, data, preferred_element_type=jnp.float32
            )
            copies.append(
                pltpu.make_async_copy(
                    value_ref.at[slot, p], out_ref.at[f, p], sems.at[2 * slot + p]
                )
            )
            copies[-1].start()
    for copy in copies:
        copy.wait()


def apply(factor_part, held, earlier=None):
    part = factor_part.shape[0]
    operands = [factor_part, held]
    aliases = {}
    if earlier is not None:
        aliases = {len(operands): 0}
        operands.append(pltpu.with_memory_space_constraint(earlier, pltpu.HBM))
    return pl.pallas_call(
        functools.partial(apply_kernel, earlier is not None),
        out_shape=pltpu.HBM(held.shape, jnp.float32),
        in_specs=whole_vmem(2) + [pl.BlockSpec(memory_space=pltpu.HBM)] * len(aliases),
        out_specs=pl.BlockSpec(memory_space=pltpu.HBM),
        scratch_shapes=[
            pltpu.VMEM((part,) + held.shape[1:], jnp.float32),
            pltpu.SemaphoreType.DMA((2 * part,)),
        ],
        input_output_aliases=aliases,
        compiler_params=pltpu.CompilerParams(vmem_limit_bytes=VMEM_LIMIT),
        name="apply",
    )(*operands)


def swap(value, size, mask):
    return lax.ppermute(value, "space", [(i, i ^ mask) for i in range(size)])


def local(snapshots, frequencies, offsets):
    halves = lax.axis_size("tm")
    size = lax.axis_size("space")
    scale = 1.0 / (snapshots.shape[2] * size)
    if halves == 2:
        mine, theirs = project(snapshots, frequencies, offsets, 2)
        pieces = [mine, lax.ppermute(theirs, "tm", [(0, 1), (1, 0)])]
        held, keep, send = gram(pieces, 2, scale)
    else:
        (coeffs,) = project(snapshots, frequencies, offsets, 1)
        regrouped = lax.all_to_all(coeffs, "tm", split_axis=0, concat_axis=2, tiled=True)
        held, keep, send = gram([regrouped], 1, scale)
    total = keep + swap(send, size, 1)
    terms = [total]
    bit = 2
    while bit < size:
        total = functools.reduce(jnp.add, terms)
        masks = [bit, 2 * bit, 3 * bit] if 2 * bit < size else [bit]
        terms = [total] + [swap(total, size, mask) for mask in masks]
        bit *= 4
    own = factor(terms)
    sent = swap(own, size, 1)
    return apply(sent, held, apply(own, held))


def solution(mesh):
    placed = (P("tm", None, "space"), P(), P("tm"))
    return jax.shard_map(
        local, mesh=mesh, in_specs=placed, out_specs=P("tm", None, None, "space"), check_vma=False
    )
```

```python
import functools
import math

import jax
import jax.numpy as jnp
from jax import lax
from jax.experimental import pallas as pl
from jax.experimental.pallas import tpu as pltpu
from jax.sharding import PartitionSpec as P

TILE = 8
CHUNK = 16
VMEM_LIMIT = 32 * 1024 * 1024


def whole_vmem(count):
    return [pl.BlockSpec(memory_space=pltpu.VMEM)] * count


def rows_of(shape):
    return lax.broadcasted_iota(jnp.int32, shape, 0)


def lanes_of(shape):
    return lax.broadcasted_iota(jnp.int32, shape, 1)


def project_kernel(groups, freq_in, offset_in, snap_ref, *refs):
    outs, tails = refs[:groups], refs[groups:-4]
    freq_ref, offset_ref, held, sems = refs[-4:]
    blocks, length, cells = snap_ref.shape
    chunks = blocks // TILE
    small = [
        pltpu.make_async_copy(freq_in, freq_ref, sems.at[chunks]),
        pltpu.make_async_copy(offset_in, offset_ref, sems.at[chunks + 1]),
    ]
    for copy in small:
        copy.start()
    copies = []
    for step in range(chunks):
        part = pl.ds(step * TILE, TILE)
        copies.append(pltpu.make_async_copy(snap_ref.at[part], held.at[part], sems.at[step]))
        copies[-1].start()

    for copy in small:
        copy.wait()
    count = freq_ref.shape[0]
    per_group = count // groups
    part = per_group // 2
    first = lax.axis_index("tm") * per_group if groups > 1 else 0
    flip = lax.rem(lax.axis_index("space"), 2) * part if groups > 1 else 0
    picked = [
        freq_ref[lax.rem(first + j - j % per_group + lax.rem(j + flip, per_group), count)]
        for j in range(count)
    ]

    def turned(moments):
        row = rows_of((2 * count, moments.shape[1]))
        freq = jnp.zeros(row.shape, jnp.int32)
        for j in range(count):
            freq = jnp.where((row == j) | (row == j + count), picked[j], freq)
        turns = lax.rem(freq * moments, length)
        turns = jnp.where(row >= count, turns - length // 4, turns)
        return jnp.cos(turns.astype(jnp.float32) * (2.0 * math.pi / length))

    moments = lanes_of((2 * count, length))
    window = 0.5 - 0.5 * jnp.cos(moments.astype(jnp.float32) * (2.0 * math.pi / length))
    table = window * turned(moments)
    tile_row = rows_of((TILE, length))
    table_rows = []
    for j in range(2 * count):
        spread = jnp.broadcast_to(table[j : j + 1, :], (TILE, length))
        table_rows.append(
            jnp.concatenate([jnp.where(tile_row == b, spread, 0.0) for b in range(TILE)], axis=1)
        )
    spread_table = jnp.concatenate(table_rows, axis=0).astype(jnp.bfloat16)
    phases = turned(jnp.broadcast_to(offset_ref[...], (2 * count, blocks))).T

    for step in range(blocks // CHUNK):
        parts = []
        for half in range(CHUNK // TILE):
            copies[step * (CHUNK // TILE) + half].wait()
        for half in range(CHUNK // TILE):
            start = step * CHUNK + half * TILE
            data = held[start : start + TILE].reshape(TILE * length, cells)
            projected = jnp.dot(spread_table, data, preferred_element_type=jnp.float32)
            turn = phases[start : start + TILE]
            pairs = []
            for j in range(count):
                cos_part = projected[j * TILE : (j + 1) * TILE]
                sin_part = projected[(count + j) * TILE : (count + j + 1) * TILE]
                cos_phase = turn[:, j : j + 1]
                sin_phase = turn[:, count + j : count + j + 1]
                pairs.append(
                    (
                        cos_part * cos_phase - sin_part * sin_phase,
                        -(sin_part * cos_phase + cos_part * sin_phase),
                    )
                )
            parts.append(pairs)
        for j in range(count):
            for p in range(2):
                value = jnp.concatenate([pairs[j][p] for pairs in parts], axis=0)
                value = value.astype(jnp.bfloat16)
                group, slot = divmod(j, per_group)
                place = slice(step * CHUNK, (step + 1) * CHUNK)
                outs[group][slot, p, place, :] = value
                if groups > 1 and slot >= part:
                    tails[group][slot - part, p, place, :] = value


def project(snapshots, frequencies, offsets, groups):
    blocks, length, cells = snapshots.shape
    count = frequencies.shape[0]
    per_group = count // groups
    shapes = [pltpu.VMEM((per_group, 2, blocks, cells), jnp.bfloat16)] * groups
    if groups > 1:
        shapes += [pltpu.VMEM((per_group // 2, 2, blocks, cells), jnp.bfloat16)] * groups
    operands = [
        pltpu.with_memory_space_constraint(operand, pltpu.HBM)
        for operand in (frequencies, offsets.reshape(1, blocks), snapshots)
    ]
    return pl.pallas_call(
        functools.partial(project_kernel, groups),
        out_shape=shapes,
        in_specs=[pl.BlockSpec(memory_space=pltpu.HBM)] * 3,
        out_specs=whole_vmem(len(shapes)),
        scratch_shapes=[
            pltpu.SMEM((count,), jnp.int32),
            pltpu.VMEM((1, blocks), jnp.int32),
            pltpu.VMEM(snapshots.shape, snapshots.dtype),
            pltpu.SemaphoreType.DMA((blocks // TILE + 2,)),
        ],
        compiler_params=pltpu.CompilerParams(vmem_limit_bytes=VMEM_LIMIT),
        name="project",
    )(*operands)


def gram_kernel(halves, scale, *refs):
    own, beside = refs[:halves], refs[halves : 2 * halves]
    held_ref, packed_ref, other = refs[2 * halves :]
    order = held_ref.shape[2]
    first = lax.axis_index("tm") if halves > 1 else 0
    size = order // halves
    for h in range(halves):
        place = pl.ds(pl.multiple_of(lax.rem(first + h, halves) * size, size), size)
        held_ref[:, :, place, :] = own[h][...]
        other[:, :, place, :] = beside[h][...]
    lower = rows_of((order, order)) >= lanes_of((order, order))
    turn = (((1,), (1,)), ((), ()))
    for f in range(other.shape[0]):
        real = jnp.concatenate([held_ref[f, 0], other[f, 0]], axis=1)
        imag = jnp.concatenate([held_ref[f, 1], other[f, 1]], axis=1)
        both = jnp.concatenate([real, imag], axis=1)
        crossed = jnp.concatenate([imag, -real], axis=1)
        gram_real = lax.dot_general(both, both, turn, preferred_element_type=jnp.float32)
        gram_imag = lax.dot_general(crossed, both, turn, preferred_element_type=jnp.float32)
        packed_ref[f] = jnp.where(lower, gram_real, gram_imag) * scale


def gram(own, beside, scale):
    halves = len(own)
    count, _, size, cells = own[0].shape
    order = size * halves
    held = jax.ShapeDtypeStruct((count, 2, order, cells), jnp.bfloat16)
    return pl.pallas_call(
        functools.partial(gram_kernel, halves, scale),
        out_shape=[held, jax.ShapeDtypeStruct((count // 2, order, order), jnp.float32)],
        in_specs=whole_vmem(2 * halves),
        out_specs=whole_vmem(2),
        scratch_shapes=[pltpu.VMEM((count // 2,) + held.shape[1:], held.dtype)],
        compiler_params=pltpu.CompilerParams(vmem_limit_bytes=VMEM_LIMIT),
        name="gram",
    )(*own, *beside)


def spread_row(tile, p):
    return jnp.broadcast_to(tile[p : p + 1, :], tile.shape)


def spread_lane(tile, p):
    return jnp.take_along_axis(tile, jnp.full(tile.shape, p, jnp.int32), axis=1)


def add_up(terms):
    while len(terms) > 1:
        pairs = [a + b for a, b in zip(terms[::2], terms[1::2])]
        terms = pairs + terms[len(pairs) * 2 :]
    return terms[0]


def column_pairs(tile, base):
    return [tuple(spread_lane(part, base + p) for part in tile) for p in range(TILE)]


def row_pairs(tile):
    return [tuple(spread_row(part, p) for part in tile) for p in range(TILE)]


def subtract_product(tile, columns, rows):
    pairs = list(zip(columns, rows))
    return (
        tile[0] - add_up([cr * rr - ci * ri for (cr, ci), (rr, ri) in pairs]),
        tile[1] - add_up([cr * ri + ci * rr for (cr, ci), (rr, ri) in pairs]),
    )


def clear_lanes(tile, low, high):
    lane = lanes_of(tile[0].shape)
    cleared = (lane >= low) & (lane < high)
    return tuple(jnp.where(cleared, 0.0, part) for part in tile)


def eliminate_tile(tile, base):
    shape = tile[0].shape
    row = rows_of(shape)
    columns = column_pairs(tile, base)
    real, imag = clear_lanes(tile, base, base + TILE)
    real = jnp.where(lanes_of(shape) == base + row, 1.0, real)
    done_real, done_imag = real, imag
    inverses = jnp.ones(shape, jnp.float32)
    for p in range(TILE):
        here = row == p
        pivot = spread_row(columns[p][0], p)
        inverse = 1.0 / pivot
        root = lax.rsqrt(pivot)
        done_real = jnp.where(here, real * root, done_real)
        done_imag = jnp.where(here, imag * root, done_imag)
        inverses = jnp.where(here, inverse, inverses)
        lead_real, lead_imag = (jnp.where(here, 0.0, part) * inverse for part in columns[p])

        def reduce_rows(a_real, a_imag):
            top_real, top_imag = spread_row(a_real, p), spread_row(a_imag, p)
            return (
                a_real - (lead_real * top_real - lead_imag * top_imag),
                a_imag - (lead_real * top_imag + lead_imag * top_real),
            )

        for q in range(p + 1, TILE):
            columns[q] = reduce_rows(*columns[q])
        real, imag = reduce_rows(real, imag)
    return (done_real, done_imag), (real * inverses, imag * inverses)


def three_parts(value):
    parts = []
    for _ in range(3):
        parts.append(value.astype(jnp.bfloat16))
        value = value - parts[-1].astype(jnp.float32)
    return parts


def outer_product(real, imag):
    reals, imags = three_parts(real), three_parts(imag)
    left = [jnp.concatenate(pair, axis=0) for pair in zip(reals, imags)]
    right = [
        jnp.concatenate(
            [jnp.concatenate([a, b], axis=1), jnp.concatenate([b, -a], axis=1)], axis=0
        )
        for a, b in zip(reals, imags)
    ]
    chosen = [(0, 0), (0, 1), (1, 0), (0, 2), (2, 0), (1, 1)]
    return lax.dot_general(
        jnp.concatenate([left[a] for a, _ in chosen], axis=0),
        jnp.concatenate([right[b] for _, b in chosen], axis=0),
        (((0,), (0,)), ((), ())),
        preferred_element_type=jnp.float32,
    )


def invert_factor(packed, out_ref, slot):
    order = packed.shape[0]
    count = order // TILE
    flipped = packed.T
    row, lane = rows_of((order, order)), lanes_of((order, order))
    full_real = jnp.where(row >= lane, packed, flipped)
    full_imag = jnp.where(row < lane, packed, jnp.where(row == lane, 0.0, -flipped))
    tiles = [
        (full_real[t * TILE : (t + 1) * TILE], full_imag[t * TILE : (t + 1) * TILE])
        for t in range(count)
    ]

    def store(done, base):
        kept = clear_lanes(done, base + TILE, order)
        out_ref[slot, 0, base : base + TILE, :] = kept[0]
        out_ref[slot, 1, base : base + TILE, :] = kept[1]

    for first in range(0, count, 2):
        second = first + 1
        base, middle, end = first * TILE, second * TILE, (second + 1) * TILE
        near = [t for t in (first + 2, first + 3) if t < count]
        columns = column_pairs(tiles[second], base)
        upper_done, upper = eliminate_tile(tiles[first], base)
        store(upper_done, base)
        tiles[second] = subtract_product(
            clear_lanes(tiles[second], base, middle), columns, row_pairs(upper)
        )
        back = column_pairs(upper, middle)
        near_columns = [
            column_pairs(tiles[t], base) + column_pairs(tiles[t], middle) for t in near
        ]
        lower_done, lower = eliminate_tile(tiles[second], middle)
        store(lower_done, middle)
        if not near:
            break
        lower_rows = row_pairs(lower)
        upper = subtract_product(clear_lanes(upper, middle, end), back, lower_rows)
        both_rows = row_pairs(upper) + lower_rows
        for t, lead in zip(near, near_columns):
            tiles[t] = subtract_product(clear_lanes(tiles[t], base, end), lead, both_rows)
        if first + 4 < count:
            upper_done = clear_lanes(upper_done, middle, end)
            change = outer_product(
                *(jnp.concatenate(pair, axis=0) for pair in zip(upper_done, lower_done))
            )
            for t in range(first + 4, count):
                real, imag = clear_lanes(tiles[t], base, end)
                part = change[t * TILE : (t + 1) * TILE]
                tiles[t] = (real - part[:, :order], imag - part[:, order:])


def factor_kernel(terms, *refs):
    out_ref = refs[terms]
    total = refs[0][...]
    for r in refs[1:terms]:
        total = total + r[...]
    for slot in range(total.shape[0]):
        invert_factor(total[slot], out_ref, slot)


def factor(terms):
    count, order, _ = terms[0].shape
    return pl.pallas_call(
        functools.partial(factor_kernel, len(terms)),
        out_shape=jax.ShapeDtypeStruct((count, 2, order, order), jnp.float32),
        in_specs=whole_vmem(len(terms)),
        out_specs=pl.BlockSpec(memory_space=pltpu.VMEM),
        compiler_params=pltpu.CompilerParams(vmem_limit_bytes=VMEM_LIMIT),
        name="factor",
    )(*terms)


def apply_kernel(other, factor_ref, held_ref, *refs):
    out_ref, value_ref, sems = refs[-3:]
    part = factor_ref.shape[0]
    bit = lax.rem(lax.axis_index("space"), 2)
    which = 1 - bit if other else bit
    copies = []
    for slot in range(part):
        f = which * part + slot
        real, imag = factor_ref[slot, 0], factor_ref[slot, 1]
        data = held_ref[part * other + slot].reshape(2 * held_ref.shape[2], held_ref.shape[3])
        for p, full in enumerate(
            (jnp.concatenate([real, -imag], axis=1), jnp.concatenate([imag, real], axis=1))
        ):
            high = full.astype(jnp.bfloat16)
            low = (full - high.astype(jnp.float32)).astype(jnp.bfloat16)
            value_ref[slot, p] = jnp.dot(high, data, preferred_element_type=jnp.float32) + jnp.dot(
                low, data, preferred_element_type=jnp.float32
            )
            copies.append(
                pltpu.make_async_copy(
                    value_ref.at[slot, p], out_ref.at[f, p], sems.at[2 * slot + p]
                )
            )
            copies[-1].start()
    for copy in copies:
        copy.wait()


def apply(factor_part, held, earlier=None):
    part = factor_part.shape[0]
    operands = [factor_part, held]
    aliases = {}
    if earlier is not None:
        aliases = {len(operands): 0}
        operands.append(pltpu.with_memory_space_constraint(earlier, pltpu.HBM))
    return pl.pallas_call(
        functools.partial(apply_kernel, earlier is not None),
        out_shape=pltpu.HBM(held.shape, jnp.float32),
        in_specs=whole_vmem(2) + [pl.BlockSpec(memory_space=pltpu.HBM)] * len(aliases),
        out_specs=pl.BlockSpec(memory_space=pltpu.HBM),
        scratch_shapes=[
            pltpu.VMEM((part,) + held.shape[1:], jnp.float32),
            pltpu.SemaphoreType.DMA((2 * part,)),
        ],
        input_output_aliases=aliases,
        compiler_params=pltpu.CompilerParams(vmem_limit_bytes=VMEM_LIMIT),
        name="apply",
    )(*operands)


def swap(value, size, mask):
    return lax.ppermute(value, "space", [(i, i ^ mask) for i in range(size)])


def swap_corner(value, size):
    pairs = [(t * size + i, (1 - t) * size + (i ^ 1)) for t in range(2) for i in range(size)]
    return lax.ppermute(value, ("tm", "space"), pairs)


def local(snapshots, frequencies, offsets):
    size = lax.axis_size("space")
    scale = 1.0 / (snapshots.shape[2] * size)
    if lax.axis_size("tm") == 2:
        mine, theirs, mine_tail, theirs_tail = project(snapshots, frequencies, offsets, 2)
        own = [mine, lax.ppermute(theirs, "tm", [(0, 1), (1, 0)])]
        beside = [swap(mine_tail, size, 1), swap_corner(theirs_tail, size)]
    else:
        (coeffs,) = project(snapshots, frequencies, offsets, 1)
        regrouped = lax.all_to_all(coeffs, "tm", split_axis=0, concat_axis=2, tiled=True)
        part = regrouped.shape[0] // 2
        flipped = jnp.roll(regrouped, part, axis=0)
        own = [jnp.where(lax.axis_index("space") % 2 == 0, regrouped, flipped)]
        beside = [swap(own[0][part:], size, 1)]
    held, total = gram(own, beside, scale)
    terms = [total]
    bit = 2
    while bit < size:
        total = functools.reduce(jnp.add, terms)
        masks = [bit, 2 * bit, 3 * bit] if 2 * bit < size else [bit]
        terms = [total] + [swap(total, size, mask) for mask in masks]
        bit *= 4
    own = factor(terms)
    sent = swap(own, size, 1)
    return apply(sent, held, apply(own, held))


def solution(mesh):
    placed = (P("tm", None, "space"), P(), P("tm"))
    return jax.shard_map(
        local, mesh=mesh, in_specs=placed, out_specs=P("tm", None, None, "space"), check_vma=False
    )
```

```python
import functools
import math

import jax
import jax.numpy as jnp
from jax import lax
from jax.experimental import pallas as pl
from jax.experimental.pallas import tpu as pltpu
from jax.sharding import PartitionSpec as P

TILE = 8
CHUNK = 16
VMEM_LIMIT = 32 * 1024 * 1024


def whole_vmem(count):
    return [pl.BlockSpec(memory_space=pltpu.VMEM)] * count


def rows_of(shape):
    return lax.broadcasted_iota(jnp.int32, shape, 0)


def lanes_of(shape):
    return lax.broadcasted_iota(jnp.int32, shape, 1)


def project_kernel(groups, freq_in, offset_in, snap_ref, *refs):
    outs = refs[:-4]
    freq_ref, offset_ref, held, sems = refs[-4:]
    blocks, length, cells = snap_ref.shape
    chunks = blocks // TILE
    small = [
        pltpu.make_async_copy(freq_in, freq_ref, sems.at[chunks]),
        pltpu.make_async_copy(offset_in, offset_ref, sems.at[chunks + 1]),
    ]
    for copy in small:
        copy.start()
    copies = []
    for step in range(chunks):
        part = pl.ds(step * TILE, TILE)
        copies.append(pltpu.make_async_copy(snap_ref.at[part], held.at[part], sems.at[step]))
        copies[-1].start()

    for copy in small:
        copy.wait()
    count = freq_ref.shape[0]
    per_group = count // groups
    part = per_group // 2
    first = lax.axis_index("tm") * per_group if groups > 1 else 0
    flip = lax.rem(lax.axis_index("space"), 2) * part if groups > 1 else 0
    picked = [
        freq_ref[lax.rem(first + j - j % per_group + lax.rem(j + flip, per_group), count)]
        for j in range(count)
    ]

    def turned(moments):
        row = rows_of((2 * count, moments.shape[1]))
        freq = jnp.zeros(row.shape, jnp.int32)
        for j in range(count):
            freq = jnp.where((row == j) | (row == j + count), picked[j], freq)
        turns = lax.rem(freq * moments, length)
        turns = jnp.where(row >= count, turns - length // 4, turns)
        return jnp.cos(turns.astype(jnp.float32) * (2.0 * math.pi / length))

    moments = lanes_of((2 * count, length))
    window = 0.5 - 0.5 * jnp.cos(moments.astype(jnp.float32) * (2.0 * math.pi / length))
    table = window * turned(moments)
    tile_row = rows_of((TILE, length))
    table_rows = []
    for j in range(2 * count):
        spread = jnp.broadcast_to(table[j : j + 1, :], (TILE, length))
        table_rows.append(
            jnp.concatenate([jnp.where(tile_row == b, spread, 0.0) for b in range(TILE)], axis=1)
        )
    spread_table = jnp.concatenate(table_rows, axis=0).astype(jnp.bfloat16)
    phases = turned(jnp.broadcast_to(offset_ref[...], (2 * count, blocks))).T

    for step in range(blocks // CHUNK):
        parts = []
        for half in range(CHUNK // TILE):
            copies[step * (CHUNK // TILE) + half].wait()
        for half in range(CHUNK // TILE):
            start = step * CHUNK + half * TILE
            data = held[start : start + TILE].reshape(TILE * length, cells)
            projected = jnp.dot(spread_table, data, preferred_element_type=jnp.float32)
            turn = phases[start : start + TILE]
            pairs = []
            for j in range(count):
                cos_part = projected[j * TILE : (j + 1) * TILE]
                sin_part = projected[(count + j) * TILE : (count + j + 1) * TILE]
                cos_phase = turn[:, j : j + 1]
                sin_phase = turn[:, count + j : count + j + 1]
                pairs.append(
                    (
                        cos_part * cos_phase - sin_part * sin_phase,
                        -(sin_part * cos_phase + cos_part * sin_phase),
                    )
                )
            parts.append(pairs)
        for j in range(count):
            for p in range(2):
                value = jnp.concatenate([pairs[j][p] for pairs in parts], axis=0)
                value = value.astype(jnp.bfloat16)
                target = outs[j * len(outs) // count]
                slot = j % (count // len(outs))
                target[slot, p, step * CHUNK : (step + 1) * CHUNK, :] = value


def project(snapshots, frequencies, offsets, groups):
    blocks, length, cells = snapshots.shape
    count = frequencies.shape[0]
    pieces = 2 * groups if groups > 1 else 1
    shapes = [pltpu.VMEM((count // pieces, 2, blocks, cells), jnp.bfloat16)] * pieces
    operands = [
        pltpu.with_memory_space_constraint(operand, pltpu.HBM)
        for operand in (frequencies, offsets.reshape(1, blocks), snapshots)
    ]
    return pl.pallas_call(
        functools.partial(project_kernel, groups),
        out_shape=shapes,
        in_specs=[pl.BlockSpec(memory_space=pltpu.HBM)] * 3,
        out_specs=whole_vmem(len(shapes)),
        scratch_shapes=[
            pltpu.SMEM((count,), jnp.int32),
            pltpu.VMEM((1, blocks), jnp.int32),
            pltpu.VMEM(snapshots.shape, snapshots.dtype),
            pltpu.SemaphoreType.DMA((blocks // TILE + 2,)),
        ],
        compiler_params=pltpu.CompilerParams(vmem_limit_bytes=VMEM_LIMIT),
        name="project",
    )(*operands)


def assemble(pieces, target):
    halves = len(pieces)
    size = pieces[0].shape[2]
    first = lax.axis_index("tm") if halves > 1 else 0
    for h, piece in enumerate(pieces):
        place = pl.ds(pl.multiple_of(lax.rem(first + h, halves) * size, size), size)
        target[:, :, place, :] = piece[...]


def gram_kernel(halves, scale, *refs):
    held_ref, packed_ref, other = refs[2 * halves :]
    order = held_ref.shape[2]
    assemble(refs[:halves], held_ref)
    assemble(refs[halves : 2 * halves], other)
    lower = rows_of((order, order)) >= lanes_of((order, order))
    turn = (((1,), (1,)), ((), ()))
    for f in range(other.shape[0]):
        real = jnp.concatenate([held_ref[f, 0], other[f, 0]], axis=1)
        imag = jnp.concatenate([held_ref[f, 1], other[f, 1]], axis=1)
        both = jnp.concatenate([real, imag], axis=1)
        crossed = jnp.concatenate([imag, -real], axis=1)
        gram_real = lax.dot_general(both, both, turn, preferred_element_type=jnp.float32)
        gram_imag = lax.dot_general(crossed, both, turn, preferred_element_type=jnp.float32)
        packed_ref[f] = jnp.where(lower, gram_real, gram_imag) * scale


def gram(own, beside, scale):
    halves = len(own)
    part, _, size, cells = own[0].shape
    order = size * halves
    held = jax.ShapeDtypeStruct((part, 2, order, cells), jnp.bfloat16)
    return pl.pallas_call(
        functools.partial(gram_kernel, halves, scale),
        out_shape=[held, jax.ShapeDtypeStruct((part, order, order), jnp.float32)],
        in_specs=whole_vmem(2 * halves),
        out_specs=whole_vmem(2),
        scratch_shapes=[pltpu.VMEM(held.shape, held.dtype)],
        compiler_params=pltpu.CompilerParams(vmem_limit_bytes=VMEM_LIMIT),
        name="gram",
    )(*own, *beside)


def spread_row(tile, p):
    return jnp.broadcast_to(tile[p : p + 1, :], tile.shape)


def spread_lane(tile, p):
    return jnp.take_along_axis(tile, jnp.full(tile.shape, p, jnp.int32), axis=1)


def add_up(terms):
    while len(terms) > 1:
        pairs = [a + b for a, b in zip(terms[::2], terms[1::2])]
        terms = pairs + terms[len(pairs) * 2 :]
    return terms[0]


def column_pairs(tile, base):
    return [tuple(spread_lane(part, base + p) for part in tile) for p in range(TILE)]


def row_pairs(tile):
    return [tuple(spread_row(part, p) for part in tile) for p in range(TILE)]


def subtract_product(tile, columns, rows):
    pairs = list(zip(columns, rows))
    return (
        tile[0] - add_up([cr * rr - ci * ri for (cr, ci), (rr, ri) in pairs]),
        tile[1] - add_up([cr * ri + ci * rr for (cr, ci), (rr, ri) in pairs]),
    )


def clear_lanes(tile, low, high):
    lane = lanes_of(tile[0].shape)
    cleared = (lane >= low) & (lane < high)
    return tuple(jnp.where(cleared, 0.0, part) for part in tile)


def eliminate_tile(tile, base):
    shape = tile[0].shape
    row = rows_of(shape)
    columns = column_pairs(tile, base)
    real, imag = clear_lanes(tile, base, base + TILE)
    real = jnp.where(lanes_of(shape) == base + row, 1.0, real)
    done_real, done_imag = real, imag
    inverses = jnp.ones(shape, jnp.float32)
    for p in range(TILE):
        here = row == p
        pivot = spread_row(columns[p][0], p)
        inverse = 1.0 / pivot
        root = lax.rsqrt(pivot)
        done_real = jnp.where(here, real * root, done_real)
        done_imag = jnp.where(here, imag * root, done_imag)
        inverses = jnp.where(here, inverse, inverses)
        lead_real, lead_imag = (jnp.where(here, 0.0, part) * inverse for part in columns[p])

        def reduce_rows(a_real, a_imag):
            top_real, top_imag = spread_row(a_real, p), spread_row(a_imag, p)
            return (
                a_real - (lead_real * top_real - lead_imag * top_imag),
                a_imag - (lead_real * top_imag + lead_imag * top_real),
            )

        for q in range(p + 1, TILE):
            columns[q] = reduce_rows(*columns[q])
        real, imag = reduce_rows(real, imag)
    return (done_real, done_imag), (real * inverses, imag * inverses)


def three_parts(value):
    parts = []
    for _ in range(3):
        parts.append(value.astype(jnp.bfloat16))
        value = value - parts[-1].astype(jnp.float32)
    return parts


def outer_product(real, imag):
    reals, imags = three_parts(real), three_parts(imag)
    left = [jnp.concatenate(pair, axis=0) for pair in zip(reals, imags)]
    right = [
        jnp.concatenate(
            [jnp.concatenate([a, b], axis=1), jnp.concatenate([b, -a], axis=1)], axis=0
        )
        for a, b in zip(reals, imags)
    ]
    chosen = [(0, 0), (0, 1), (1, 0), (0, 2), (2, 0), (1, 1)]
    return lax.dot_general(
        jnp.concatenate([left[a] for a, _ in chosen], axis=0),
        jnp.concatenate([right[b] for _, b in chosen], axis=0),
        (((0,), (0,)), ((), ())),
        preferred_element_type=jnp.float32,
    )


def invert_factor(packed, out_ref, slot):
    order = packed.shape[0]
    count = order // TILE
    flipped = packed.T
    row, lane = rows_of((order, order)), lanes_of((order, order))
    full_real = jnp.where(row >= lane, packed, flipped)
    full_imag = jnp.where(row < lane, packed, jnp.where(row == lane, 0.0, -flipped))
    tiles = [
        (full_real[t * TILE : (t + 1) * TILE], full_imag[t * TILE : (t + 1) * TILE])
        for t in range(count)
    ]

    def store(done, base):
        kept = clear_lanes(done, base + TILE, order)
        out_ref[slot, 0, base : base + TILE, :] = kept[0]
        out_ref[slot, 1, base : base + TILE, :] = kept[1]

    for first in range(0, count, 2):
        second = first + 1
        base, middle, end = first * TILE, second * TILE, (second + 1) * TILE
        near = [t for t in (first + 2, first + 3) if t < count]
        columns = column_pairs(tiles[second], base)
        upper_done, upper = eliminate_tile(tiles[first], base)
        store(upper_done, base)
        tiles[second] = subtract_product(
            clear_lanes(tiles[second], base, middle), columns, row_pairs(upper)
        )
        back = column_pairs(upper, middle)
        near_columns = [
            column_pairs(tiles[t], base) + column_pairs(tiles[t], middle) for t in near
        ]
        lower_done, lower = eliminate_tile(tiles[second], middle)
        store(lower_done, middle)
        if not near:
            break
        lower_rows = row_pairs(lower)
        upper = subtract_product(clear_lanes(upper, middle, end), back, lower_rows)
        both_rows = row_pairs(upper) + lower_rows
        for t, lead in zip(near, near_columns):
            tiles[t] = subtract_product(clear_lanes(tiles[t], base, end), lead, both_rows)
        if first + 4 < count:
            upper_done = clear_lanes(upper_done, middle, end)
            change = outer_product(
                *(jnp.concatenate(pair, axis=0) for pair in zip(upper_done, lower_done))
            )
            for t in range(first + 4, count):
                real, imag = clear_lanes(tiles[t], base, end)
                part = change[t * TILE : (t + 1) * TILE]
                tiles[t] = (real - part[:, :order], imag - part[:, order:])


def factor_kernel(terms, *refs):
    out_ref = refs[terms]
    total = refs[0][...]
    for r in refs[1:terms]:
        total = total + r[...]
    for slot in range(total.shape[0]):
        invert_factor(total[slot], out_ref, slot)


def factor(terms):
    count, order, _ = terms[0].shape
    return pl.pallas_call(
        functools.partial(factor_kernel, len(terms)),
        out_shape=jax.ShapeDtypeStruct((count, 2, order, order), jnp.float32),
        in_specs=whole_vmem(len(terms)),
        out_specs=pl.BlockSpec(memory_space=pltpu.VMEM),
        compiler_params=pltpu.CompilerParams(vmem_limit_bytes=VMEM_LIMIT),
        name="factor",
    )(*terms)


def apply_kernel(other, halves, factor_ref, *refs):
    out_ref, data_ref, value_ref, sems = refs[-4:]
    assemble(refs[:halves], data_ref)
    part, _, order, cells = data_ref.shape
    bit = lax.rem(lax.axis_index("space"), 2)
    which = 1 - bit if other else bit
    copies = []
    for slot in range(part):
        f = which * part + slot
        real, imag = factor_ref[slot, 0], factor_ref[slot, 1]
        data = data_ref[slot].reshape(2 * order, cells)
        for p, full in enumerate(
            (jnp.concatenate([real, -imag], axis=1), jnp.concatenate([imag, real], axis=1))
        ):
            high = full.astype(jnp.bfloat16)
            low = (full - high.astype(jnp.float32)).astype(jnp.bfloat16)
            value_ref[slot, p] = jnp.dot(high, data, preferred_element_type=jnp.float32) + jnp.dot(
                low, data, preferred_element_type=jnp.float32
            )
            copies.append(
                pltpu.make_async_copy(
                    value_ref.at[slot, p], out_ref.at[f, p], sems.at[2 * slot + p]
                )
            )
            copies[-1].start()
    for copy in copies:
        copy.wait()


def apply(factor_part, pieces, earlier=None):
    halves = len(pieces)
    part, _, size, cells = pieces[0].shape
    order = size * halves
    operands = [factor_part, *pieces]
    aliases = {}
    if earlier is not None:
        aliases = {len(operands): 0}
        operands.append(pltpu.with_memory_space_constraint(earlier, pltpu.HBM))
    return pl.pallas_call(
        functools.partial(apply_kernel, earlier is not None, halves),
        out_shape=pltpu.HBM((2 * part, 2, order, cells), jnp.float32),
        in_specs=whole_vmem(1 + halves) + [pl.BlockSpec(memory_space=pltpu.HBM)] * len(aliases),
        out_specs=pl.BlockSpec(memory_space=pltpu.HBM),
        scratch_shapes=[
            pltpu.VMEM((part, 2, order, cells), jnp.bfloat16),
            pltpu.VMEM((part, 2, order, cells), jnp.float32),
            pltpu.SemaphoreType.DMA((2 * part,)),
        ],
        input_output_aliases=aliases,
        compiler_params=pltpu.CompilerParams(vmem_limit_bytes=VMEM_LIMIT),
        name="apply",
    )(*operands)


def swap(value, size, mask):
    return lax.ppermute(value, "space", [(i, i ^ mask) for i in range(size)])


def swap_tm(value):
    return lax.ppermute(value, "tm", [(0, 1), (1, 0)])


def swap_corner(value, size):
    pairs = [(t * size + i, (1 - t) * size + (i ^ 1)) for t in range(2) for i in range(size)]
    return lax.ppermute(value, ("tm", "space"), pairs)


def local(snapshots, frequencies, offsets):
    size = lax.axis_size("space")
    scale = 1.0 / (snapshots.shape[2] * size)
    if lax.axis_size("tm") == 2:
        mine, mine_tail, theirs, theirs_tail = project(snapshots, frequencies, offsets, 2)
        own = [mine, swap_tm(theirs)]
        beside = [swap(mine_tail, size, 1), swap_corner(theirs_tail, size)]
        rest = [mine_tail, swap_tm(theirs_tail)]
    else:
        (coeffs,) = project(snapshots, frequencies, offsets, 1)
        regrouped = lax.all_to_all(coeffs, "tm", split_axis=0, concat_axis=2, tiled=True)
        part = regrouped.shape[0] // 2
        flipped = jnp.roll(regrouped, part, axis=0)
        ordered = jnp.where(lax.axis_index("space") % 2 == 0, regrouped, flipped)
        own, rest = [ordered[:part]], [ordered[part:]]
        beside = [swap(rest[0], size, 1)]
    held, total = gram(own, beside, scale)
    terms = [total]
    bit = 2
    while bit < size:
        total = functools.reduce(jnp.add, terms)
        masks = [bit, 2 * bit, 3 * bit] if 2 * bit < size else [bit]
        terms = [total] + [swap(total, size, mask) for mask in masks]
        bit *= 4
    terms, rest = lax.optimization_barrier((terms, rest))
    own = factor(terms)
    sent = swap(own, size, 1)
    return apply(sent, rest, apply(own, [held]))


def solution(mesh):
    placed = (P("tm", None, "space"), P(), P("tm"))
    return jax.shard_map(
        local, mesh=mesh, in_specs=placed, out_specs=P("tm", None, None, "space"), check_vma=False
    )
```

```python
import functools
import math

import jax
import jax.numpy as jnp
from jax import lax
from jax.experimental import pallas as pl
from jax.experimental.pallas import tpu as pltpu
from jax.sharding import PartitionSpec as P

TILE = 8
CHUNK = 16
VMEM_LIMIT = 32 * 1024 * 1024


def whole_vmem(count):
    return [pl.BlockSpec(memory_space=pltpu.VMEM)] * count


def rows_of(shape):
    return lax.broadcasted_iota(jnp.int32, shape, 0)


def lanes_of(shape):
    return lax.broadcasted_iota(jnp.int32, shape, 1)


def project_kernel(groups, freq_in, offset_in, snap_ref, *refs):
    outs = refs[:-4]
    freq_ref, offset_ref, held, sems = refs[-4:]
    blocks, length, cells = snap_ref.shape
    chunks = blocks // TILE
    small = [
        pltpu.make_async_copy(freq_in, freq_ref, sems.at[chunks]),
        pltpu.make_async_copy(offset_in, offset_ref, sems.at[chunks + 1]),
    ]
    for copy in small:
        copy.start()
    copies = []
    for step in range(chunks):
        part = pl.ds(step * TILE, TILE)
        copies.append(pltpu.make_async_copy(snap_ref.at[part], held.at[part], sems.at[step]))
        copies[-1].start()

    for copy in small:
        copy.wait()
    count = freq_ref.shape[0]
    per_group = count // groups
    part = per_group // 2
    first = lax.axis_index("tm") * per_group if groups > 1 else 0
    flip = lax.rem(lax.axis_index("space"), 2) * part if groups > 1 else 0
    picked = [
        freq_ref[lax.rem(first + j - j % per_group + lax.rem(j + flip, per_group), count)]
        for j in range(count)
    ]

    def turned(moments):
        row = rows_of((2 * count, moments.shape[1]))
        freq = jnp.zeros(row.shape, jnp.int32)
        for j in range(count):
            freq = jnp.where((row == j) | (row == j + count), picked[j], freq)
        turns = lax.rem(freq * moments, length)
        turns = jnp.where(row >= count, turns - length // 4, turns)
        return jnp.cos(turns.astype(jnp.float32) * (2.0 * math.pi / length))

    moments = lanes_of((2 * count, length))
    window = 0.5 - 0.5 * jnp.cos(moments.astype(jnp.float32) * (2.0 * math.pi / length))
    table = window * turned(moments)
    tile_row = rows_of((TILE, length))
    table_rows = []
    for j in range(2 * count):
        spread = jnp.broadcast_to(table[j : j + 1, :], (TILE, length))
        table_rows.append(
            jnp.concatenate([jnp.where(tile_row == b, spread, 0.0) for b in range(TILE)], axis=1)
        )
    spread_table = jnp.concatenate(table_rows, axis=0).astype(jnp.bfloat16)
    phases = turned(jnp.broadcast_to(offset_ref[...], (2 * count, blocks))).T

    for step in range(blocks // CHUNK):
        parts = []
        for half in range(CHUNK // TILE):
            copies[step * (CHUNK // TILE) + half].wait()
        for half in range(CHUNK // TILE):
            start = step * CHUNK + half * TILE
            data = held[start : start + TILE].reshape(TILE * length, cells)
            projected = jnp.dot(spread_table, data, preferred_element_type=jnp.float32)
            turn = phases[start : start + TILE]
            pairs = []
            for j in range(count):
                cos_part = projected[j * TILE : (j + 1) * TILE]
                sin_part = projected[(count + j) * TILE : (count + j + 1) * TILE]
                cos_phase = turn[:, j : j + 1]
                sin_phase = turn[:, count + j : count + j + 1]
                pairs.append(
                    (
                        cos_part * cos_phase - sin_part * sin_phase,
                        -(sin_part * cos_phase + cos_part * sin_phase),
                    )
                )
            parts.append(pairs)
        for j in range(count):
            for p in range(2):
                value = jnp.concatenate([pairs[j][p] for pairs in parts], axis=0)
                value = value.astype(jnp.bfloat16)
                target = outs[j * len(outs) // count]
                slot = j % (count // len(outs))
                target[slot, p, step * CHUNK : (step + 1) * CHUNK, :] = value


def project(snapshots, frequencies, offsets, groups):
    blocks, length, cells = snapshots.shape
    count = frequencies.shape[0]
    pieces = 2 * groups if groups > 1 else 1
    shapes = [pltpu.VMEM((count // pieces, 2, blocks, cells), jnp.bfloat16)] * pieces
    operands = [
        pltpu.with_memory_space_constraint(operand, pltpu.HBM)
        for operand in (frequencies, offsets.reshape(1, blocks), snapshots)
    ]
    return pl.pallas_call(
        functools.partial(project_kernel, groups),
        out_shape=shapes,
        in_specs=[pl.BlockSpec(memory_space=pltpu.HBM)] * 3,
        out_specs=whole_vmem(len(shapes)),
        scratch_shapes=[
            pltpu.SMEM((count,), jnp.int32),
            pltpu.VMEM((1, blocks), jnp.int32),
            pltpu.VMEM(snapshots.shape, snapshots.dtype),
            pltpu.SemaphoreType.DMA((blocks // TILE + 2,)),
        ],
        compiler_params=pltpu.CompilerParams(vmem_limit_bytes=VMEM_LIMIT),
        name="project",
    )(*operands)


def assemble(pieces, target):
    halves = len(pieces)
    size = pieces[0].shape[2]
    first = lax.axis_index("tm") if halves > 1 else 0
    for h, piece in enumerate(pieces):
        place = pl.ds(pl.multiple_of(lax.rem(first + h, halves) * size, size), size)
        target[:, :, place, :] = piece[...]


def gram_kernel(halves, scale, *refs):
    held_ref, packed_ref, other = refs[2 * halves :]
    order = held_ref.shape[2]
    assemble(refs[:halves], held_ref)
    assemble(refs[halves : 2 * halves], other)
    lower = rows_of((order, order)) >= lanes_of((order, order))
    turn = (((1,), (1,)), ((), ()))
    for f in range(other.shape[0]):
        real = jnp.concatenate([held_ref[f, 0], other[f, 0]], axis=1)
        imag = jnp.concatenate([held_ref[f, 1], other[f, 1]], axis=1)
        both = jnp.concatenate([real, imag], axis=1)
        crossed = jnp.concatenate([imag, -real], axis=1)
        gram_real = lax.dot_general(both, both, turn, preferred_element_type=jnp.float32)
        gram_imag = lax.dot_general(crossed, both, turn, preferred_element_type=jnp.float32)
        packed_ref[f] = jnp.where(lower, gram_real, gram_imag) * scale


def gram(own, beside, scale):
    halves = len(own)
    part, _, size, cells = own[0].shape
    order = size * halves
    held = jax.ShapeDtypeStruct((part, 2, order, cells), jnp.bfloat16)
    return pl.pallas_call(
        functools.partial(gram_kernel, halves, scale),
        out_shape=[held, jax.ShapeDtypeStruct((part, order, order), jnp.float32)],
        in_specs=whole_vmem(2 * halves),
        out_specs=whole_vmem(2),
        scratch_shapes=[pltpu.VMEM(held.shape, held.dtype)],
        compiler_params=pltpu.CompilerParams(vmem_limit_bytes=VMEM_LIMIT),
        name="gram",
    )(*own, *beside)


def spread_row(tile, p):
    return jnp.broadcast_to(tile[p : p + 1, :], tile.shape)


def spread_lane(tile, p):
    return jnp.take_along_axis(tile, jnp.full(tile.shape, p, jnp.int32), axis=1)


def add_up(terms):
    while len(terms) > 1:
        pairs = [a + b for a, b in zip(terms[::2], terms[1::2])]
        terms = pairs + terms[len(pairs) * 2 :]
    return terms[0]


def column_pairs(tile, base):
    return [tuple(spread_lane(part, base + p) for part in tile) for p in range(TILE)]


def row_pairs(tile):
    return [tuple(spread_row(part, p) for part in tile) for p in range(TILE)]


def subtract_product(tile, columns, rows):
    pairs = list(zip(columns, rows))
    return (
        tile[0] - add_up([cr * rr - ci * ri for (cr, ci), (rr, ri) in pairs]),
        tile[1] - add_up([cr * ri + ci * rr for (cr, ci), (rr, ri) in pairs]),
    )


def clear_lanes(tile, low, high):
    lane = lanes_of(tile[0].shape)
    cleared = (lane >= low) & (lane < high)
    return tuple(jnp.where(cleared, 0.0, part) for part in tile)


def eliminate_tile(tile, base):
    shape = tile[0].shape
    row = rows_of(shape)
    columns = column_pairs(tile, base)
    real, imag = clear_lanes(tile, base, base + TILE)
    real = jnp.where(lanes_of(shape) == base + row, 1.0, real)
    done_real, done_imag = real, imag
    inverses = jnp.ones(shape, jnp.float32)
    for p in range(TILE):
        here = row == p
        pivot = spread_row(columns[p][0], p)
        inverse = 1.0 / pivot
        root = lax.rsqrt(pivot)
        done_real = jnp.where(here, real * root, done_real)
        done_imag = jnp.where(here, imag * root, done_imag)
        inverses = jnp.where(here, inverse, inverses)
        lead_real, lead_imag = (jnp.where(here, 0.0, part) * inverse for part in columns[p])

        def reduce_rows(a_real, a_imag):
            top_real, top_imag = spread_row(a_real, p), spread_row(a_imag, p)
            return (
                a_real - (lead_real * top_real - lead_imag * top_imag),
                a_imag - (lead_real * top_imag + lead_imag * top_real),
            )

        for q in range(p + 1, TILE):
            columns[q] = reduce_rows(*columns[q])
        real, imag = reduce_rows(real, imag)
    return (done_real, done_imag), (real * inverses, imag * inverses)


def three_parts(value):
    parts = []
    for _ in range(3):
        parts.append(value.astype(jnp.bfloat16))
        value = value - parts[-1].astype(jnp.float32)
    return parts


def outer_product(real, imag):
    reals, imags = three_parts(real), three_parts(imag)
    left = [jnp.concatenate(pair, axis=0) for pair in zip(reals, imags)]
    right = [
        jnp.concatenate(
            [jnp.concatenate([a, b], axis=1), jnp.concatenate([b, -a], axis=1)], axis=0
        )
        for a, b in zip(reals, imags)
    ]
    chosen = [(0, 0), (0, 1), (1, 0), (0, 2), (2, 0), (1, 1)]
    return lax.dot_general(
        jnp.concatenate([left[a] for a, _ in chosen], axis=0),
        jnp.concatenate([right[b] for _, b in chosen], axis=0),
        (((0,), (0,)), ((), ())),
        preferred_element_type=jnp.float32,
    )


def invert_factor(packed, out_ref, slot):
    order = packed.shape[0]
    count = order // TILE
    flipped = packed.T
    row, lane = rows_of((order, order)), lanes_of((order, order))
    full_real = jnp.where(row >= lane, packed, flipped)
    full_imag = jnp.where(row < lane, packed, jnp.where(row == lane, 0.0, -flipped))
    tiles = [
        (full_real[t * TILE : (t + 1) * TILE], full_imag[t * TILE : (t + 1) * TILE])
        for t in range(count)
    ]

    def store(done, base):
        kept = clear_lanes(done, base + TILE, order)
        out_ref[slot, 0, base : base + TILE, :] = kept[0]
        out_ref[slot, 1, base : base + TILE, :] = kept[1]

    for first in range(0, count, 2):
        second = first + 1
        base, middle, end = first * TILE, second * TILE, (second + 1) * TILE
        near = [t for t in (first + 2, first + 3) if t < count]
        columns = column_pairs(tiles[second], base)
        upper_done, upper = eliminate_tile(tiles[first], base)
        store(upper_done, base)
        tiles[second] = subtract_product(
            clear_lanes(tiles[second], base, middle), columns, row_pairs(upper)
        )
        back = column_pairs(upper, middle)
        near_columns = [
            column_pairs(tiles[t], base) + column_pairs(tiles[t], middle) for t in near
        ]
        lower_done, lower = eliminate_tile(tiles[second], middle)
        store(lower_done, middle)
        if not near:
            break
        lower_rows = row_pairs(lower)
        upper = subtract_product(clear_lanes(upper, middle, end), back, lower_rows)
        both_rows = row_pairs(upper) + lower_rows
        for t, lead in zip(near, near_columns):
            tiles[t] = subtract_product(clear_lanes(tiles[t], base, end), lead, both_rows)
        if first + 4 < count:
            upper_done = clear_lanes(upper_done, middle, end)
            change = outer_product(
                *(jnp.concatenate(pair, axis=0) for pair in zip(upper_done, lower_done))
            )
            for t in range(first + 4, count):
                real, imag = clear_lanes(tiles[t], base, end)
                part = change[t * TILE : (t + 1) * TILE]
                tiles[t] = (real - part[:, :order], imag - part[:, order:])


def factor_kernel(terms, *refs):
    out_ref = refs[-1]
    total = refs[0][...]
    for r in refs[1:terms]:
        total = total + r[...]
    for slot in range(total.shape[0]):
        invert_factor(total[slot], out_ref, slot)


def factor(terms, beside):
    count, order, _ = terms[0].shape
    return pl.pallas_call(
        functools.partial(factor_kernel, len(terms)),
        out_shape=jax.ShapeDtypeStruct((count, 2, order, order), jnp.float32),
        in_specs=whole_vmem(len(terms)) + [pl.BlockSpec(memory_space=pl.ANY)] * len(beside),
        out_specs=pl.BlockSpec(memory_space=pltpu.VMEM),
        compiler_params=pltpu.CompilerParams(vmem_limit_bytes=VMEM_LIMIT),
        name="factor",
    )(*terms, *beside)


def apply_kernel(other, halves, factor_ref, *refs):
    out_ref, data_ref, value_ref, sems = refs[-4:]
    assemble(refs[:halves], data_ref)
    part, _, order, cells = data_ref.shape
    bit = lax.rem(lax.axis_index("space"), 2)
    which = 1 - bit if other else bit
    copies = []
    for slot in range(part):
        f = which * part + slot
        real, imag = factor_ref[slot, 0], factor_ref[slot, 1]
        data = data_ref[slot].reshape(2 * order, cells)
        for p, full in enumerate(
            (jnp.concatenate([real, -imag], axis=1), jnp.concatenate([imag, real], axis=1))
        ):
            high = full.astype(jnp.bfloat16)
            low = (full - high.astype(jnp.float32)).astype(jnp.bfloat16)
            value_ref[slot, p] = jnp.dot(high, data, preferred_element_type=jnp.float32) + jnp.dot(
                low, data, preferred_element_type=jnp.float32
            )
            copies.append(
                pltpu.make_async_copy(
                    value_ref.at[slot, p], out_ref.at[f, p], sems.at[2 * slot + p]
                )
            )
            copies[-1].start()
    for copy in copies:
        copy.wait()


def apply(factor_part, pieces, earlier=None):
    halves = len(pieces)
    part, _, size, cells = pieces[0].shape
    order = size * halves
    operands = [factor_part, *pieces]
    aliases = {}
    if earlier is not None:
        aliases = {len(operands): 0}
        operands.append(pltpu.with_memory_space_constraint(earlier, pltpu.HBM))
    return pl.pallas_call(
        functools.partial(apply_kernel, earlier is not None, halves),
        out_shape=pltpu.HBM((2 * part, 2, order, cells), jnp.float32),
        in_specs=whole_vmem(1 + halves) + [pl.BlockSpec(memory_space=pltpu.HBM)] * len(aliases),
        out_specs=pl.BlockSpec(memory_space=pltpu.HBM),
        scratch_shapes=[
            pltpu.VMEM((part, 2, order, cells), jnp.bfloat16),
            pltpu.VMEM((part, 2, order, cells), jnp.float32),
            pltpu.SemaphoreType.DMA((2 * part,)),
        ],
        input_output_aliases=aliases,
        compiler_params=pltpu.CompilerParams(vmem_limit_bytes=VMEM_LIMIT),
        name="apply",
    )(*operands)


def swap(value, size, mask):
    return lax.ppermute(value, "space", [(i, i ^ mask) for i in range(size)])


def swap_tm(value):
    return lax.ppermute(value, "tm", [(0, 1), (1, 0)])


def swap_corner(value, size):
    pairs = [(t * size + i, (1 - t) * size + (i ^ 1)) for t in range(2) for i in range(size)]
    return lax.ppermute(value, ("tm", "space"), pairs)


def local(snapshots, frequencies, offsets):
    size = lax.axis_size("space")
    scale = 1.0 / (snapshots.shape[2] * size)
    if lax.axis_size("tm") == 2:
        mine, mine_tail, theirs, theirs_tail = project(snapshots, frequencies, offsets, 2)
        own = [mine, swap_tm(theirs)]
        beside = [swap(mine_tail, size, 1), swap_corner(theirs_tail, size)]
        rest = [mine_tail, swap(beside[1], size, 1)]
        alive = [theirs_tail]
    else:
        (coeffs,) = project(snapshots, frequencies, offsets, 1)
        regrouped = lax.all_to_all(coeffs, "tm", split_axis=0, concat_axis=2, tiled=True)
        part = regrouped.shape[0] // 2
        flipped = jnp.roll(regrouped, part, axis=0)
        ordered = jnp.where(lax.axis_index("space") % 2 == 0, regrouped, flipped)
        own, rest = [ordered[:part]], [ordered[part:]]
        beside = [swap(rest[0], size, 1)]
        alive = []
    held, total = gram(own, beside, scale)
    terms = [total]
    bit = 2
    while bit < size:
        total = functools.reduce(jnp.add, terms)
        masks = [bit, 2 * bit, 3 * bit] if 2 * bit < size else [bit]
        terms = [total] + [swap(total, size, mask) for mask in masks]
        bit *= 4
    terms, rest = lax.optimization_barrier((terms, rest))
    own = factor(terms, alive)
    sent = swap(own, size, 1)
    return apply(sent, rest, apply(own, [held]))


def solution(mesh):
    placed = (P("tm", None, "space"), P(), P("tm"))
    return jax.shard_map(
        local, mesh=mesh, in_specs=placed, out_specs=P("tm", None, None, "space"), check_vma=False
    )
```

```python
import functools
import math

import jax
import jax.numpy as jnp
from jax import lax
from jax.experimental import pallas as pl
from jax.experimental.pallas import tpu as pltpu
from jax.sharding import PartitionSpec as P

TILE = 8
CHUNK = 16
VMEM_LIMIT = 32 * 1024 * 1024


def whole_vmem(count):
    return [pl.BlockSpec(memory_space=pltpu.VMEM)] * count


def rows_of(shape):
    return lax.broadcasted_iota(jnp.int32, shape, 0)


def lanes_of(shape):
    return lax.broadcasted_iota(jnp.int32, shape, 1)


def project_kernel(groups, freq_in, offset_in, snap_ref, *refs):
    outs = refs[:-4]
    freq_ref, offset_ref, held, sems = refs[-4:]
    blocks, length, cells = snap_ref.shape
    chunks = blocks // TILE
    small = [
        pltpu.make_async_copy(freq_in, freq_ref, sems.at[chunks]),
        pltpu.make_async_copy(offset_in, offset_ref, sems.at[chunks + 1]),
    ]
    for copy in small:
        copy.start()
    copies = []
    for step in range(chunks):
        part = pl.ds(step * TILE, TILE)
        copies.append(pltpu.make_async_copy(snap_ref.at[part], held.at[part], sems.at[step]))
        copies[-1].start()

    for copy in small:
        copy.wait()
    count = freq_ref.shape[0]
    per_group = count // groups
    part = per_group // 2
    first = lax.axis_index("tm") * per_group if groups > 1 else 0
    flip = lax.rem(lax.axis_index("space"), 2) * part if groups > 1 else 0
    picked = [
        freq_ref[lax.rem(first + j - j % per_group + lax.rem(j + flip, per_group), count)]
        for j in range(count)
    ]

    def turned(moments):
        row = rows_of((2 * count, moments.shape[1]))
        freq = jnp.zeros(row.shape, jnp.int32)
        for j in range(count):
            freq = jnp.where((row == j) | (row == j + count), picked[j], freq)
        turns = lax.rem(freq * moments, length)
        turns = jnp.where(row >= count, turns - length // 4, turns)
        return jnp.cos(turns.astype(jnp.float32) * (2.0 * math.pi / length))

    moments = lanes_of((2 * count, length))
    window = 0.5 - 0.5 * jnp.cos(moments.astype(jnp.float32) * (2.0 * math.pi / length))
    table = window * turned(moments)
    tile_row = rows_of((TILE, length))
    table_rows = []
    for j in range(2 * count):
        spread = jnp.broadcast_to(table[j : j + 1, :], (TILE, length))
        table_rows.append(
            jnp.concatenate([jnp.where(tile_row == b, spread, 0.0) for b in range(TILE)], axis=1)
        )
    spread_table = jnp.concatenate(table_rows, axis=0).astype(jnp.bfloat16)
    phases = turned(jnp.broadcast_to(offset_ref[...], (2 * count, blocks))).T

    for step in range(blocks // CHUNK):
        parts = []
        for half in range(CHUNK // TILE):
            copies[step * (CHUNK // TILE) + half].wait()
        for half in range(CHUNK // TILE):
            start = step * CHUNK + half * TILE
            data = held[start : start + TILE].reshape(TILE * length, cells)
            projected = jnp.dot(spread_table, data, preferred_element_type=jnp.float32)
            turn = phases[start : start + TILE]
            pairs = []
            for j in range(count):
                cos_part = projected[j * TILE : (j + 1) * TILE]
                sin_part = projected[(count + j) * TILE : (count + j + 1) * TILE]
                cos_phase = turn[:, j : j + 1]
                sin_phase = turn[:, count + j : count + j + 1]
                pairs.append(
                    (
                        cos_part * cos_phase - sin_part * sin_phase,
                        -(sin_part * cos_phase + cos_part * sin_phase),
                    )
                )
            parts.append(pairs)
        for j in range(count):
            for p in range(2):
                value = jnp.concatenate([pairs[j][p] for pairs in parts], axis=0)
                value = value.astype(jnp.bfloat16)
                target = outs[j * len(outs) // count]
                slot = j % (count // len(outs))
                target[slot, p, step * CHUNK : (step + 1) * CHUNK, :] = value


def project(snapshots, frequencies, offsets, groups):
    blocks, length, cells = snapshots.shape
    count = frequencies.shape[0]
    pieces = 2 * groups if groups > 1 else 1
    shapes = [pltpu.VMEM((count // pieces, 2, blocks, cells), jnp.bfloat16)] * pieces
    operands = [
        pltpu.with_memory_space_constraint(operand, pltpu.HBM)
        for operand in (frequencies, offsets.reshape(1, blocks), snapshots)
    ]
    return pl.pallas_call(
        functools.partial(project_kernel, groups),
        out_shape=shapes,
        in_specs=[pl.BlockSpec(memory_space=pltpu.HBM)] * 3,
        out_specs=whole_vmem(len(shapes)),
        scratch_shapes=[
            pltpu.SMEM((count,), jnp.int32),
            pltpu.VMEM((1, blocks), jnp.int32),
            pltpu.VMEM(snapshots.shape, snapshots.dtype),
            pltpu.SemaphoreType.DMA((blocks // TILE + 2,)),
        ],
        compiler_params=pltpu.CompilerParams(vmem_limit_bytes=VMEM_LIMIT),
        name="project",
    )(*operands)


def assemble(pieces, target):
    halves = len(pieces)
    size = pieces[0].shape[2]
    first = lax.axis_index("tm") if halves > 1 else 0
    for h, piece in enumerate(pieces):
        place = pl.ds(pl.multiple_of(lax.rem(first + h, halves) * size, size), size)
        target[:, :, place, :] = piece[...]


def gram_kernel(halves, scale, *refs):
    held_ref, packed_ref, other = refs[2 * halves :]
    order = held_ref.shape[2]
    assemble(refs[:halves], held_ref)
    assemble(refs[halves : 2 * halves], other)
    lower = rows_of((order, order)) >= lanes_of((order, order))
    turn = (((1,), (1,)), ((), ()))
    for f in range(other.shape[0]):
        real = jnp.concatenate([held_ref[f, 0], other[f, 0]], axis=1)
        imag = jnp.concatenate([held_ref[f, 1], other[f, 1]], axis=1)
        both = jnp.concatenate([real, imag], axis=1)
        crossed = jnp.concatenate([imag, -real], axis=1)
        gram_real = lax.dot_general(both, both, turn, preferred_element_type=jnp.float32)
        gram_imag = lax.dot_general(crossed, both, turn, preferred_element_type=jnp.float32)
        packed_ref[f] = jnp.where(lower, gram_real, gram_imag) * scale


def gram(own, beside, scale):
    halves = len(own)
    part, _, size, cells = own[0].shape
    order = size * halves
    held = jax.ShapeDtypeStruct((part, 2, order, cells), jnp.bfloat16)
    return pl.pallas_call(
        functools.partial(gram_kernel, halves, scale),
        out_shape=[held, jax.ShapeDtypeStruct((part, order, order), jnp.float32)],
        in_specs=whole_vmem(2 * halves),
        out_specs=whole_vmem(2),
        scratch_shapes=[pltpu.VMEM(held.shape, held.dtype)],
        compiler_params=pltpu.CompilerParams(vmem_limit_bytes=VMEM_LIMIT),
        name="gram",
    )(*own, *beside)


def spread_row(tile, p):
    return jnp.broadcast_to(tile[p : p + 1, :], tile.shape)


def spread_lane(tile, p):
    return jnp.take_along_axis(tile, jnp.full(tile.shape, p, jnp.int32), axis=1)


def add_up(terms):
    while len(terms) > 1:
        pairs = [a + b for a, b in zip(terms[::2], terms[1::2])]
        terms = pairs + terms[len(pairs) * 2 :]
    return terms[0]


def column_pairs(tile, base):
    return [tuple(spread_lane(part, base + p) for part in tile) for p in range(TILE)]


def row_pairs(tile):
    return [tuple(spread_row(part, p) for part in tile) for p in range(TILE)]


def subtract_product(tile, columns, rows):
    pairs = list(zip(columns, rows))
    return (
        tile[0] - add_up([cr * rr - ci * ri for (cr, ci), (rr, ri) in pairs]),
        tile[1] - add_up([cr * ri + ci * rr for (cr, ci), (rr, ri) in pairs]),
    )


def clear_lanes(tile, low, high):
    lane = lanes_of(tile[0].shape)
    cleared = (lane >= low) & (lane < high)
    return tuple(jnp.where(cleared, 0.0, part) for part in tile)


def eliminate_tile(tile, base):
    shape = tile[0].shape
    row = rows_of(shape)
    columns = column_pairs(tile, base)
    real, imag = clear_lanes(tile, base, base + TILE)
    real = jnp.where(lanes_of(shape) == base + row, 1.0, real)
    done_real, done_imag = real, imag
    inverses = jnp.ones(shape, jnp.float32)
    for p in range(TILE):
        here = row == p
        pivot = spread_row(columns[p][0], p)
        inverse = 1.0 / pivot
        root = lax.rsqrt(pivot)
        done_real = jnp.where(here, real * root, done_real)
        done_imag = jnp.where(here, imag * root, done_imag)
        inverses = jnp.where(here, inverse, inverses)
        lead_real, lead_imag = (jnp.where(here, 0.0, part) * inverse for part in columns[p])

        def reduce_rows(a_real, a_imag):
            top_real, top_imag = spread_row(a_real, p), spread_row(a_imag, p)
            return (
                a_real - (lead_real * top_real - lead_imag * top_imag),
                a_imag - (lead_real * top_imag + lead_imag * top_real),
            )

        for q in range(p + 1, TILE):
            columns[q] = reduce_rows(*columns[q])
        real, imag = reduce_rows(real, imag)
    return (done_real, done_imag), (real * inverses, imag * inverses)


def three_parts(value):
    parts = []
    for _ in range(3):
        parts.append(value.astype(jnp.bfloat16))
        value = value - parts[-1].astype(jnp.float32)
    return parts


def outer_product(real, imag):
    reals, imags = three_parts(real), three_parts(imag)
    left = [jnp.concatenate(pair, axis=0) for pair in zip(reals, imags)]
    right = [
        jnp.concatenate(
            [jnp.concatenate([a, b], axis=1), jnp.concatenate([b, -a], axis=1)], axis=0
        )
        for a, b in zip(reals, imags)
    ]
    chosen = [(0, 0), (0, 1), (1, 0), (0, 2), (2, 0), (1, 1)]
    return lax.dot_general(
        jnp.concatenate([left[a] for a, _ in chosen], axis=0),
        jnp.concatenate([right[b] for _, b in chosen], axis=0),
        (((0,), (0,)), ((), ())),
        preferred_element_type=jnp.float32,
    )


def invert_factor(packed, out_ref, slot):
    order = packed.shape[0]
    count = order // TILE
    flipped = packed.T
    row, lane = rows_of((order, order)), lanes_of((order, order))
    full_real = jnp.where(row >= lane, packed, flipped)
    full_imag = jnp.where(row < lane, packed, jnp.where(row == lane, 0.0, -flipped))
    tiles = [
        (full_real[t * TILE : (t + 1) * TILE], full_imag[t * TILE : (t + 1) * TILE])
        for t in range(count)
    ]

    def store(done, base):
        kept = clear_lanes(done, base + TILE, order)
        out_ref[slot, 0, base : base + TILE, :] = kept[0]
        out_ref[slot, 1, base : base + TILE, :] = kept[1]

    for first in range(0, count, 2):
        second = first + 1
        base, middle, end = first * TILE, second * TILE, (second + 1) * TILE
        near = [t for t in (first + 2, first + 3) if t < count]
        columns = column_pairs(tiles[second], base)
        upper_done, upper = eliminate_tile(tiles[first], base)
        store(upper_done, base)
        tiles[second] = subtract_product(
            clear_lanes(tiles[second], base, middle), columns, row_pairs(upper)
        )
        back = column_pairs(upper, middle)
        near_columns = [
            column_pairs(tiles[t], base) + column_pairs(tiles[t], middle) for t in near
        ]
        lower_done, lower = eliminate_tile(tiles[second], middle)
        store(lower_done, middle)
        if not near:
            break
        lower_rows = row_pairs(lower)
        upper = subtract_product(clear_lanes(upper, middle, end), back, lower_rows)
        both_rows = row_pairs(upper) + lower_rows
        for t, lead in zip(near, near_columns):
            tiles[t] = subtract_product(clear_lanes(tiles[t], base, end), lead, both_rows)
        if first + 4 < count:
            upper_done = clear_lanes(upper_done, middle, end)
            change = outer_product(
                *(jnp.concatenate(pair, axis=0) for pair in zip(upper_done, lower_done))
            )
            for t in range(first + 4, count):
                real, imag = clear_lanes(tiles[t], base, end)
                part = change[t * TILE : (t + 1) * TILE]
                tiles[t] = (real - part[:, :order], imag - part[:, order:])


def factor_kernel(terms, *refs):
    out_ref = refs[terms]
    total = refs[0][...]
    for r in refs[1:terms]:
        total = total + r[...]
    for slot in range(total.shape[0]):
        invert_factor(total[slot], out_ref, slot)


def factor(terms):
    count, order, _ = terms[0].shape
    return pl.pallas_call(
        functools.partial(factor_kernel, len(terms)),
        out_shape=jax.ShapeDtypeStruct((count, 2, order, order), jnp.float32),
        in_specs=whole_vmem(len(terms)),
        out_specs=pl.BlockSpec(memory_space=pltpu.VMEM),
        compiler_params=pltpu.CompilerParams(vmem_limit_bytes=VMEM_LIMIT),
        name="factor",
    )(*terms)


def apply_kernel(other, later, factor_ref, data_ref, *refs):
    value_ref, sems = refs[-2:]
    if other:
        out_ref = refs[-3]
    else:
        out_ref, later_ref = refs[-4:-2]
        assemble(refs[:later], later_ref)
    part, _, order, cells = data_ref.shape
    bit = lax.rem(lax.axis_index("space"), 2)
    which = 1 - bit if other else bit
    copies = []
    for slot in range(part):
        f = which * part + slot
        real, imag = factor_ref[slot, 0], factor_ref[slot, 1]
        data = data_ref[slot].reshape(2 * order, cells)
        for p, full in enumerate(
            (jnp.concatenate([real, -imag], axis=1), jnp.concatenate([imag, real], axis=1))
        ):
            high = full.astype(jnp.bfloat16)
            low = (full - high.astype(jnp.float32)).astype(jnp.bfloat16)
            value_ref[slot, p] = jnp.dot(high, data, preferred_element_type=jnp.float32) + jnp.dot(
                low, data, preferred_element_type=jnp.float32
            )
            copies.append(
                pltpu.make_async_copy(
                    value_ref.at[slot, p], out_ref.at[f, p], sems.at[2 * slot + p]
                )
            )
            copies[-1].start()
    for copy in copies:
        copy.wait()


def apply(factor_part, held, later=(), earlier=None):
    part, _, order, cells = held.shape
    operands = [factor_part, held, *later]
    shapes = [pltpu.HBM((2 * part, 2, order, cells), jnp.float32)]
    in_specs = whole_vmem(len(operands))
    out_specs = [pl.BlockSpec(memory_space=pltpu.HBM)]
    aliases = {}
    if earlier is not None:
        aliases = {len(operands): 0}
        operands.append(pltpu.with_memory_space_constraint(earlier, pltpu.HBM))
        in_specs += out_specs
    else:
        shapes.append(pltpu.VMEM(held.shape, held.dtype))
        out_specs = out_specs + whole_vmem(1)
    return pl.pallas_call(
        functools.partial(apply_kernel, earlier is not None, len(later)),
        out_shape=shapes,
        in_specs=in_specs,
        out_specs=out_specs,
        scratch_shapes=[
            pltpu.VMEM((part, 2, order, cells), jnp.float32),
            pltpu.SemaphoreType.DMA((2 * part,)),
        ],
        input_output_aliases=aliases,
        compiler_params=pltpu.CompilerParams(vmem_limit_bytes=VMEM_LIMIT),
        name="apply",
    )(*operands)


def swap(value, size, mask):
    return lax.ppermute(value, "space", [(i, i ^ mask) for i in range(size)])


def swap_tm(value):
    return lax.ppermute(value, "tm", [(0, 1), (1, 0)])


def swap_corner(value, size):
    pairs = [(t * size + i, (1 - t) * size + (i ^ 1)) for t in range(2) for i in range(size)]
    return lax.ppermute(value, ("tm", "space"), pairs)


def local(snapshots, frequencies, offsets):
    size = lax.axis_size("space")
    scale = 1.0 / (snapshots.shape[2] * size)
    if lax.axis_size("tm") == 2:
        mine, mine_tail, theirs, theirs_tail = project(snapshots, frequencies, offsets, 2)
        own = [mine, swap_tm(theirs)]
        beside = [swap(mine_tail, size, 1), swap_corner(theirs_tail, size)]
        rest = [mine_tail, swap_tm(theirs_tail)]
    else:
        (coeffs,) = project(snapshots, frequencies, offsets, 1)
        regrouped = lax.all_to_all(coeffs, "tm", split_axis=0, concat_axis=2, tiled=True)
        part = regrouped.shape[0] // 2
        flipped = jnp.roll(regrouped, part, axis=0)
        ordered = jnp.where(lax.axis_index("space") % 2 == 0, regrouped, flipped)
        own, rest = [ordered[:part]], [ordered[part:]]
        beside = [swap(rest[0], size, 1)]
    held, total = gram(own, beside, scale)
    terms = [total]
    bit = 2
    while bit < size:
        total = functools.reduce(jnp.add, terms)
        masks = [bit, 2 * bit, 3 * bit] if 2 * bit < size else [bit]
        terms = [total] + [swap(total, size, mask) for mask in masks]
        bit *= 4
    terms, rest = lax.optimization_barrier((terms, rest))
    own = factor(terms)
    sent = swap(own, size, 1)
    modes, held_rest = apply(own, held, rest)
    return apply(sent, held_rest, earlier=modes)[0]


def solution(mesh):
    placed = (P("tm", None, "space"), P(), P("tm"))
    return jax.shard_map(
        local, mesh=mesh, in_specs=placed, out_specs=P("tm", None, None, "space"), check_vma=False
    )
```

```python
import functools
import math

import jax
import jax.numpy as jnp
from jax import lax
from jax.experimental import pallas as pl
from jax.experimental.pallas import tpu as pltpu
from jax.sharding import PartitionSpec as P

TILE = 8
CHUNK = 16
VMEM_LIMIT = 32 * 1024 * 1024


def whole_vmem(count):
    return [pl.BlockSpec(memory_space=pltpu.VMEM)] * count


def rows_of(shape):
    return lax.broadcasted_iota(jnp.int32, shape, 0)


def lanes_of(shape):
    return lax.broadcasted_iota(jnp.int32, shape, 1)


def project_kernel(groups, freq_in, offset_in, snap_ref, *refs):
    outs = refs[:-4]
    freq_ref, offset_ref, held, sems = refs[-4:]
    blocks, length, cells = snap_ref.shape
    chunks = blocks // TILE
    small = [
        pltpu.make_async_copy(freq_in, freq_ref, sems.at[chunks]),
        pltpu.make_async_copy(offset_in, offset_ref, sems.at[chunks + 1]),
    ]
    for copy in small:
        copy.start()
    copies = []
    for step in range(chunks):
        part = pl.ds(step * TILE, TILE)
        copies.append(pltpu.make_async_copy(snap_ref.at[part], held.at[part], sems.at[step]))
        copies[-1].start()

    for copy in small:
        copy.wait()
    count = freq_ref.shape[0]
    per_group = count // groups
    part = per_group // 2
    first = lax.axis_index("tm") * per_group if groups > 1 else 0
    flip = lax.rem(lax.axis_index("space"), 2) * part if groups > 1 else 0
    picked = [
        freq_ref[lax.rem(first + j - j % per_group + lax.rem(j + flip, per_group), count)]
        for j in range(count)
    ]

    def turned(moments):
        row = rows_of((2 * count, moments.shape[1]))
        freq = jnp.zeros(row.shape, jnp.int32)
        for j in range(count):
            freq = jnp.where((row == j) | (row == j + count), picked[j], freq)
        turns = lax.rem(freq * moments, length)
        turns = jnp.where(row >= count, turns - length // 4, turns)
        return jnp.cos(turns.astype(jnp.float32) * (2.0 * math.pi / length))

    moments = lanes_of((2 * count, length))
    window = 0.5 - 0.5 * jnp.cos(moments.astype(jnp.float32) * (2.0 * math.pi / length))
    table = window * turned(moments)
    tile_row = rows_of((TILE, length))
    table_rows = []
    for j in range(2 * count):
        spread = jnp.broadcast_to(table[j : j + 1, :], (TILE, length))
        table_rows.append(
            jnp.concatenate([jnp.where(tile_row == b, spread, 0.0) for b in range(TILE)], axis=1)
        )
    spread_table = jnp.concatenate(table_rows, axis=0).astype(jnp.bfloat16)
    phases = turned(jnp.broadcast_to(offset_ref[...], (2 * count, blocks))).T

    for step in range(blocks // CHUNK):
        parts = []
        for half in range(CHUNK // TILE):
            copies[step * (CHUNK // TILE) + half].wait()
        for half in range(CHUNK // TILE):
            start = step * CHUNK + half * TILE
            data = held[start : start + TILE].reshape(TILE * length, cells)
            projected = jnp.dot(spread_table, data, preferred_element_type=jnp.float32)
            turn = phases[start : start + TILE]
            pairs = []
            for j in range(count):
                cos_part = projected[j * TILE : (j + 1) * TILE]
                sin_part = projected[(count + j) * TILE : (count + j + 1) * TILE]
                cos_phase = turn[:, j : j + 1]
                sin_phase = turn[:, count + j : count + j + 1]
                pairs.append(
                    (
                        cos_part * cos_phase - sin_part * sin_phase,
                        -(sin_part * cos_phase + cos_part * sin_phase),
                    )
                )
            parts.append(pairs)
        for j in range(count):
            for p in range(2):
                value = jnp.concatenate([pairs[j][p] for pairs in parts], axis=0)
                value = value.astype(jnp.bfloat16)
                target = outs[j * len(outs) // count]
                slot = j % (count // len(outs))
                target[slot, p, step * CHUNK : (step + 1) * CHUNK, :] = value


def project(snapshots, frequencies, offsets, groups):
    blocks, length, cells = snapshots.shape
    count = frequencies.shape[0]
    pieces = 2 * groups if groups > 1 else 1
    shapes = [pltpu.VMEM((count // pieces, 2, blocks, cells), jnp.bfloat16)] * pieces
    operands = [
        pltpu.with_memory_space_constraint(operand, pltpu.HBM)
        for operand in (frequencies, offsets.reshape(1, blocks), snapshots)
    ]
    return pl.pallas_call(
        functools.partial(project_kernel, groups),
        out_shape=shapes,
        in_specs=[pl.BlockSpec(memory_space=pltpu.HBM)] * 3,
        out_specs=whole_vmem(len(shapes)),
        scratch_shapes=[
            pltpu.SMEM((count,), jnp.int32),
            pltpu.VMEM((1, blocks), jnp.int32),
            pltpu.VMEM(snapshots.shape, snapshots.dtype),
            pltpu.SemaphoreType.DMA((blocks // TILE + 2,)),
        ],
        compiler_params=pltpu.CompilerParams(vmem_limit_bytes=VMEM_LIMIT),
        name="project",
    )(*operands)


def assemble(pieces, target):
    halves = len(pieces)
    size = pieces[0].shape[2]
    first = lax.axis_index("tm") if halves > 1 else 0
    for h, piece in enumerate(pieces):
        place = pl.ds(pl.multiple_of(lax.rem(first + h, halves) * size, size), size)
        target[:, :, place, :] = piece[...]


def gram_kernel(halves, scale, *refs):
    held_ref, packed_ref, other = refs[2 * halves :]
    order = held_ref.shape[2]
    assemble(refs[:halves], held_ref)
    assemble(refs[halves : 2 * halves], other)
    lower = rows_of((order, order)) >= lanes_of((order, order))
    turn = (((1,), (1,)), ((), ()))
    for f in range(other.shape[0]):
        real = jnp.concatenate([held_ref[f, 0], other[f, 0]], axis=1)
        imag = jnp.concatenate([held_ref[f, 1], other[f, 1]], axis=1)
        both = jnp.concatenate([real, imag], axis=1)
        crossed = jnp.concatenate([imag, -real], axis=1)
        gram_real = lax.dot_general(both, both, turn, preferred_element_type=jnp.float32)
        gram_imag = lax.dot_general(crossed, both, turn, preferred_element_type=jnp.float32)
        packed_ref[f] = jnp.where(lower, gram_real, gram_imag) * scale


def gram(own, beside, scale):
    halves = len(own)
    part, _, size, cells = own[0].shape
    order = size * halves
    held = jax.ShapeDtypeStruct((part, 2, order, cells), jnp.bfloat16)
    return pl.pallas_call(
        functools.partial(gram_kernel, halves, scale),
        out_shape=[held, jax.ShapeDtypeStruct((part, order, order), jnp.float32)],
        in_specs=whole_vmem(2 * halves),
        out_specs=whole_vmem(2),
        scratch_shapes=[pltpu.VMEM(held.shape, held.dtype)],
        compiler_params=pltpu.CompilerParams(vmem_limit_bytes=VMEM_LIMIT),
        name="gram",
    )(*own, *beside)


def spread_row(tile, p):
    return jnp.broadcast_to(tile[p : p + 1, :], tile.shape)


def spread_lane(tile, p):
    return jnp.take_along_axis(tile, jnp.full(tile.shape, p, jnp.int32), axis=1)


def add_up(terms):
    while len(terms) > 1:
        pairs = [a + b for a, b in zip(terms[::2], terms[1::2])]
        terms = pairs + terms[len(pairs) * 2 :]
    return terms[0]


def column_pairs(tile, base):
    return [tuple(spread_lane(part, base + p) for part in tile) for p in range(TILE)]


def row_pairs(tile):
    return [tuple(spread_row(part, p) for part in tile) for p in range(TILE)]


def subtract_product(tile, columns, rows):
    pairs = list(zip(columns, rows))
    return (
        tile[0] - add_up([cr * rr - ci * ri for (cr, ci), (rr, ri) in pairs]),
        tile[1] - add_up([cr * ri + ci * rr for (cr, ci), (rr, ri) in pairs]),
    )


def clear_lanes(tile, low, high):
    lane = lanes_of(tile[0].shape)
    cleared = (lane >= low) & (lane < high)
    return tuple(jnp.where(cleared, 0.0, part) for part in tile)


def eliminate_tile(tile, base):
    shape = tile[0].shape
    row = rows_of(shape)
    columns = column_pairs(tile, base)
    real, imag = clear_lanes(tile, base, base + TILE)
    real = jnp.where(lanes_of(shape) == base + row, 1.0, real)
    done_real, done_imag = real, imag
    inverses = jnp.ones(shape, jnp.float32)
    for p in range(TILE):
        here = row == p
        pivot = spread_row(columns[p][0], p)
        inverse = 1.0 / pivot
        root = lax.rsqrt(pivot)
        done_real = jnp.where(here, real * root, done_real)
        done_imag = jnp.where(here, imag * root, done_imag)
        inverses = jnp.where(here, inverse, inverses)
        lead_real, lead_imag = (jnp.where(here, 0.0, part) * inverse for part in columns[p])

        def reduce_rows(a_real, a_imag):
            top_real, top_imag = spread_row(a_real, p), spread_row(a_imag, p)
            return (
                a_real - (lead_real * top_real - lead_imag * top_imag),
                a_imag - (lead_real * top_imag + lead_imag * top_real),
            )

        for q in range(p + 1, TILE):
            columns[q] = reduce_rows(*columns[q])
        real, imag = reduce_rows(real, imag)
    return (done_real, done_imag), (real * inverses, imag * inverses)


def three_parts(value):
    parts = []
    for _ in range(3):
        parts.append(value.astype(jnp.bfloat16))
        value = value - parts[-1].astype(jnp.float32)
    return parts


def outer_product(real, imag):
    reals, imags = three_parts(real), three_parts(imag)
    left = [jnp.concatenate(pair, axis=0) for pair in zip(reals, imags)]
    right = [
        jnp.concatenate(
            [jnp.concatenate([a, b], axis=1), jnp.concatenate([b, -a], axis=1)], axis=0
        )
        for a, b in zip(reals, imags)
    ]
    chosen = [(0, 0), (0, 1), (1, 0), (0, 2), (2, 0), (1, 1)]
    return lax.dot_general(
        jnp.concatenate([left[a] for a, _ in chosen], axis=0),
        jnp.concatenate([right[b] for _, b in chosen], axis=0),
        (((0,), (0,)), ((), ())),
        preferred_element_type=jnp.float32,
    )


def invert_factor(packed, out_ref, slot):
    order = packed.shape[0]
    count = order // TILE
    flipped = packed.T
    row, lane = rows_of((order, order)), lanes_of((order, order))
    full_real = jnp.where(row >= lane, packed, flipped)
    full_imag = jnp.where(row < lane, packed, jnp.where(row == lane, 0.0, -flipped))
    tiles = [
        (full_real[t * TILE : (t + 1) * TILE], full_imag[t * TILE : (t + 1) * TILE])
        for t in range(count)
    ]

    def store(done, base):
        kept = clear_lanes(done, base + TILE, order)
        out_ref[slot, 0, base : base + TILE, :] = kept[0]
        out_ref[slot, 1, base : base + TILE, :] = kept[1]

    for first in range(0, count, 2):
        second = first + 1
        base, middle, end = first * TILE, second * TILE, (second + 1) * TILE
        near = [t for t in (first + 2, first + 3) if t < count]
        columns = column_pairs(tiles[second], base)
        upper_done, upper = eliminate_tile(tiles[first], base)
        store(upper_done, base)
        tiles[second] = subtract_product(
            clear_lanes(tiles[second], base, middle), columns, row_pairs(upper)
        )
        back = column_pairs(upper, middle)
        near_columns = [
            column_pairs(tiles[t], base) + column_pairs(tiles[t], middle) for t in near
        ]
        lower_done, lower = eliminate_tile(tiles[second], middle)
        store(lower_done, middle)
        if not near:
            break
        lower_rows = row_pairs(lower)
        upper = subtract_product(clear_lanes(upper, middle, end), back, lower_rows)
        both_rows = row_pairs(upper) + lower_rows
        for t, lead in zip(near, near_columns):
            tiles[t] = subtract_product(clear_lanes(tiles[t], base, end), lead, both_rows)
        if first + 4 < count:
            upper_done = clear_lanes(upper_done, middle, end)
            change = outer_product(
                *(jnp.concatenate(pair, axis=0) for pair in zip(upper_done, lower_done))
            )
            for t in range(first + 4, count):
                real, imag = clear_lanes(tiles[t], base, end)
                part = change[t * TILE : (t + 1) * TILE]
                tiles[t] = (real - part[:, :order], imag - part[:, order:])


def factor_kernel(terms, *refs):
    out_ref = refs[-1]
    total = refs[0][...]
    for r in refs[1:terms]:
        total = total + r[...]
    for slot in range(total.shape[0]):
        invert_factor(total[slot], out_ref, slot)


def factor(terms, alive):
    count, order, _ = terms[0].shape
    return pl.pallas_call(
        functools.partial(factor_kernel, len(terms)),
        out_shape=jax.ShapeDtypeStruct((count, 2, order, order), jnp.float32),
        in_specs=whole_vmem(len(terms)) + [pl.BlockSpec(memory_space=pl.ANY)] * len(alive),
        out_specs=pl.BlockSpec(memory_space=pltpu.VMEM),
        compiler_params=pltpu.CompilerParams(vmem_limit_bytes=VMEM_LIMIT),
        name="factor",
    )(*terms, *alive)


def apply_kernel(other, later, factor_ref, data_ref, *refs):
    value_ref, sems = refs[-2:]
    if other:
        out_ref = refs[-3]
    else:
        out_ref, later_ref = refs[-4:-2]
        assemble(refs[:later], later_ref)
    part, _, order, cells = data_ref.shape
    bit = lax.rem(lax.axis_index("space"), 2)
    which = 1 - bit if other else bit
    copies = []
    for slot in range(part):
        f = which * part + slot
        real, imag = factor_ref[slot, 0], factor_ref[slot, 1]
        data = data_ref[slot].reshape(2 * order, cells)
        for p, full in enumerate(
            (jnp.concatenate([real, -imag], axis=1), jnp.concatenate([imag, real], axis=1))
        ):
            high = full.astype(jnp.bfloat16)
            low = (full - high.astype(jnp.float32)).astype(jnp.bfloat16)
            value_ref[slot, p] = jnp.dot(high, data, preferred_element_type=jnp.float32) + jnp.dot(
                low, data, preferred_element_type=jnp.float32
            )
            copies.append(
                pltpu.make_async_copy(
                    value_ref.at[slot, p], out_ref.at[f, p], sems.at[2 * slot + p]
                )
            )
            copies[-1].start()
    for copy in copies:
        copy.wait()


def apply(factor_part, held, later=(), earlier=None):
    part, _, order, cells = held.shape
    operands = [factor_part, held, *later]
    shapes = [pltpu.HBM((2 * part, 2, order, cells), jnp.float32)]
    in_specs = whole_vmem(len(operands))
    out_specs = [pl.BlockSpec(memory_space=pltpu.HBM)]
    aliases = {}
    if earlier is not None:
        aliases = {len(operands): 0}
        operands.append(pltpu.with_memory_space_constraint(earlier, pltpu.HBM))
        in_specs += out_specs
    else:
        shapes.append(pltpu.VMEM(held.shape, held.dtype))
        out_specs = out_specs + whole_vmem(1)
    return pl.pallas_call(
        functools.partial(apply_kernel, earlier is not None, len(later)),
        out_shape=shapes,
        in_specs=in_specs,
        out_specs=out_specs,
        scratch_shapes=[
            pltpu.VMEM((part, 2, order, cells), jnp.float32),
            pltpu.SemaphoreType.DMA((2 * part,)),
        ],
        input_output_aliases=aliases,
        compiler_params=pltpu.CompilerParams(vmem_limit_bytes=VMEM_LIMIT),
        name="apply",
    )(*operands)


def swap(value, size, mask):
    return lax.ppermute(value, "space", [(i, i ^ mask) for i in range(size)])


def swap_tm(value):
    return lax.ppermute(value, "tm", [(0, 1), (1, 0)])


def swap_corner(value, size):
    pairs = [(t * size + i, (1 - t) * size + (i ^ 1)) for t in range(2) for i in range(size)]
    return lax.ppermute(value, ("tm", "space"), pairs)


def local(snapshots, frequencies, offsets):
    size = lax.axis_size("space")
    scale = 1.0 / (snapshots.shape[2] * size)
    if lax.axis_size("tm") == 2:
        mine, mine_tail, theirs, theirs_tail = project(snapshots, frequencies, offsets, 2)
        own = [mine, swap_tm(theirs)]
        beside = [swap(mine_tail, size, 1), swap_corner(theirs_tail, size)]
        rest = [mine_tail, swap(beside[1], size, 1)]
        alive = [theirs_tail]
    else:
        (coeffs,) = project(snapshots, frequencies, offsets, 1)
        regrouped = lax.all_to_all(coeffs, "tm", split_axis=0, concat_axis=2, tiled=True)
        part = regrouped.shape[0] // 2
        flipped = jnp.roll(regrouped, part, axis=0)
        ordered = jnp.where(lax.axis_index("space") % 2 == 0, regrouped, flipped)
        own, rest = [ordered[:part]], [ordered[part:]]
        beside = [swap(rest[0], size, 1)]
        alive = []
    held, total = gram(own, beside, scale)
    terms = [total]
    bit = 2
    while bit < size:
        total = functools.reduce(jnp.add, terms)
        masks = [bit, 2 * bit, 3 * bit] if 2 * bit < size else [bit]
        terms = [total] + [swap(total, size, mask) for mask in masks]
        bit *= 4
    terms, rest = lax.optimization_barrier((terms, rest))
    own = factor(terms, alive)
    sent = swap(own, size, 1)
    modes, held_rest = apply(own, held, rest)
    return apply(sent, held_rest, earlier=modes)[0]


def solution(mesh):
    placed = (P("tm", None, "space"), P(), P("tm"))
    return jax.shard_map(
        local, mesh=mesh, in_specs=placed, out_specs=P("tm", None, None, "space"), check_vma=False
    )
```
